32 devices in a mesh: gx: 4 (over x, core), gy: 4 (over z), gz: 2 (over y).
Axes of the slice: x: 2, y: 2, z: 4, core: 2. Of those that a mesh axis runs over, the one named last changes fastest.
Arguments:
- field: float32 [2, 32, 256, 512], P(None, 'gz', 'gx', 'gy'), may hold values from -30 to 30
- transfer: float32 [4, 128], replicated, may hold values from 0.2 to 3
- light_angles: float32 [2], replicated, may hold values from -3.140625 to 3.140625
Outputs:
- image: float32 [4, 256, 512], P(None, ('gx', 'gz'), 'gy')
The draws below stay inside these ranges and needn't reach their ends.
All inputs are finite; a program needn't handle non-finite values.
Results may differ from the reference program's by a relative error of at most 0.00019.
Values sent between devices are 32-bit elements; how exact they have to be, the bound alone decides.
A program may use at most 64 MiB of HBM per device.

```python
import math
import jax
import jax.numpy as jnp
from jax import lax

BINS = 128
NX = 256
NY = 512
NZ = 32


def draw_field(key, part):
    shape = (2, NZ, NX, NY)
    values = jax.random.normal(key, shape, jnp.float32) * 6.0
    return jnp.clip(values, -30.0, 30.0)


def setup_inputs(seed: int = 0) -> dict:
    arg_keys = jax.random.split(jax.random.key(seed), 4)
    field = draw_field(jax.random.fold_in(arg_keys[3], 71), 0)
    transfer = jnp.clip(jax.random.uniform(arg_keys[1], (4, BINS), jnp.float32, 0.2, 3.0), 0.2, 3.0)
    light_angles = jnp.clip(jax.random.uniform(arg_keys[2], (2,), jnp.float32, -3.140625, 3.140625), -3.140625, 3.140625)
    return dict(field=field, transfer=transfer, light_angles=light_angles)


SIGMA_TAPS = 1.2
OPTICAL = 2.0
SHADE_FLOOR = 0.25


def filter_taps():
    places = [-3, -2, -1, 0, 1, 2, 3]
    bell = [math.exp(-place * place / (2.0 * SIGMA_TAPS * SIGMA_TAPS)) for place in places]
    bell_total = sum(bell)
    slope_total = sum(place * place * weight for place, weight in zip(places, bell))
    smooth_taps = [weight / bell_total for weight in bell]
    slope_taps = [place * weight / slope_total for place, weight in zip(places, bell)]
    return smooth_taps, slope_taps


def sweep(volume, taps, axis_dim):
    length = volume.shape[axis_dim] - 6
    total = taps[0] * lax.slice_in_dim(volume, 0, length, axis=axis_dim)
    for place in range(1, 7):
        total = total + taps[place] * lax.slice_in_dim(volume, place, place + length, axis=axis_dim)
    return total


def depth_section(first, second):
    smooth_taps, slope_taps = filter_taps()
    return sweep(first, smooth_taps, 0), sweep(first, slope_taps, 0), sweep(second, smooth_taps, 0)


def cross_section(plain, slope, other):
    smooth_taps, slope_taps = filter_taps()
    return (sweep(plain, smooth_taps, 1), sweep(plain, slope_taps, 1),
            sweep(slope, smooth_taps, 1), sweep(other, smooth_taps, 1))


def row_section(plain, cross_slope, depth_slope, other):
    smooth_taps, slope_taps = filter_taps()
    value = sweep(plain, smooth_taps, 2)
    grad_y = sweep(plain, slope_taps, 2)
    grad_x = sweep(cross_slope, smooth_taps, 2)
    grad_z = sweep(depth_slope, smooth_taps, 2)
    mixture = sweep(other, smooth_taps, 2)
    return value, mixture, grad_x, grad_y, grad_z


def sample_plane(value, mixture, grad_x, grad_y, grad_z, transfer, light_angles, depth_step):
    bins = transfer.shape[1]
    position = jax.nn.sigmoid(value) * (bins - 1)
    centers = jnp.arange(bins).astype(position.dtype)
    tent = jnp.maximum(0.0, 1.0 - jnp.abs(position[None] - centers[:, None, None]))
    looked = jnp.einsum("cb,bxy->cxy", transfer, tent, precision=lax.Precision.HIGHEST)
    light_x = jnp.cos(light_angles[0]) * jnp.sin(light_angles[1])
    light_y = jnp.sin(light_angles[0]) * jnp.sin(light_angles[1])
    light_z = jnp.cos(light_angles[1])
    facing = grad_x * light_x + grad_y * light_y + grad_z * light_z
    diffuse = facing * facing / (grad_x * grad_x + grad_y * grad_y + grad_z * grad_z + SHADE_FLOOR)
    shade = 0.25 + 0.75 * diffuse
    alpha = 1.0 - jnp.exp(-OPTICAL * looked[3] * jax.nn.sigmoid(mixture) * depth_step)
    return jnp.concatenate([(alpha * shade)[None] * looked[:3], alpha[None]], 0)


def over(front, back):
    return front + (1.0 - front[3:4]) * back


def integrate(value, mixture, grad_x, grad_y, grad_z, transfer, light_angles, depth_step):
    def advance(running, planes):
        sample = sample_plane(planes[0], planes[1], planes[2], planes[3], planes[4],
                              transfer, light_angles, depth_step)
        return over(running, sample), None

    start = jnp.zeros((4,) + value.shape[1:], value.dtype)
    result, unused = lax.scan(advance, start, (value, mixture, grad_x, grad_y, grad_z))
    return result


def reference(field, transfer, light_angles):
    padded = jnp.pad(field, ((0, 0), (3, 3), (3, 3), (3, 3)))
    plain, slope, other = depth_section(padded[0], padded[1])
    cross_plain, cross_slope, depth_slope, cross_other = cross_section(plain, slope, other)
    value, mixture, grad_x, grad_y, grad_z = row_section(cross_plain, cross_slope, depth_slope, cross_other)
    return integrate(value, mixture, grad_x, grad_y, grad_z, transfer, light_angles, 1.0 / NZ)
```

```python
import functools
import math

import jax
import jax.numpy as jnp
from jax import lax
from jax.experimental import pallas as pl
from jax.experimental.pallas import tpu as pltpu
from jax.sharding import PartitionSpec as P

MESH = pl.DeviceIdType.MESH
SIGMA_TAPS = 1.2
OPTICAL = 2.0
SHADE_FLOOR = 0.25
EDGE = 8


def filter_taps():
    places = [-3, -2, -1, 0, 1, 2, 3]
    bell = [math.exp(-place * place / (2.0 * SIGMA_TAPS * SIGMA_TAPS)) for place in places]
    bell_total = sum(bell)
    slope_total = sum((place * place * weight for place, weight in zip(places, bell)))
    smooth_taps = [weight / bell_total for weight in bell]
    slope_taps = [place * weight / slope_total for place, weight in zip(places, bell)]
    return (smooth_taps, slope_taps)


def smooth_of(at):
    taps, _ = filter_taps()
    total = taps[3] * at(0)
    for o in (1, 2, 3):
        total = total + taps[3 + o] * (at(o) + at(-o))
    return total


def slope_of(at):
    _, taps = filter_taps()
    total = taps[4] * (at(1) - at(-1))
    for o in (2, 3):
        total = total + taps[3 + o] * (at(o) - at(-o))
    return total


def both_of(at):
    smooth, slope = filter_taps()
    plain, steep = smooth[3] * at(0), None
    for o in (1, 2, 3):
        after, before = at(o), at(-o)
        plain = plain + smooth[3 + o] * (after + before)
        term = slope[3 + o] * (after - before)
        steep = term if steep is None else steep + term
    return plain, steep


def kernel(sizes, depth_step, field, transfer, angles, out, box, own_strips, rim_strips, got_own, got_rim,
           rows_done, flat_done, table, light, inner, stage, slabs,
           local_sem, send_sem, recv_sem, slab_send, slab_recv):
    nx, ny, nz = sizes
    _, depth, rows, lanes = field.shape
    total = rows + 2 * EDGE
    ix, iy, iz = (lax.axis_index(name) for name in ("gx", "gy", "gz"))
    spots = {"gx": (ix, nx), "gy": (iy, ny), "gz": (iz, nz)}

    def has(axis, step):
        place, count = spots[axis]
        return place > 0 if step < 0 else place < count - 1

    def target(axis, step):
        return {axis: spots[axis][0] + step}

    barrier = pltpu.get_barrier_semaphore()
    for axis in ("gx", "gy"):
        for step in (-1, 1):
            @pl.when(has(axis, step))
            def _():
                pl.semaphore_signal(barrier, inc=1, device_id=target(axis, step), device_id_type=MESH)
    for j in range(1, nz):
        pl.semaphore_signal(barrier, inc=1, device_id={"gz": lax.rem(iz + j, nz)}, device_id_type=MESH)

    own = pltpu.make_async_copy(
        field, box.at[:, pl.ds(3, depth), pl.ds(EDGE, rows), :], local_sem)
    own.start()

    for step in (-1, 1):
        edge = 0 if step < 0 else EDGE + rows
        @pl.when(jnp.logical_not(has("gx", step)))
        def _():
            box[:, :, edge:edge + EDGE, :] = jnp.zeros((2, depth + 6, EDGE, lanes), jnp.float32)
        first = 0 if step < 0 else depth + 3
        @pl.when(jnp.logical_not(has("gz", step)))
        def _():
            box[:, first:first + 3] = jnp.zeros((2, 3, total, lanes), jnp.float32)
        side = 0 if step < 0 else 1
        @pl.when(jnp.logical_not(has("gy", step)))
        def _():
            got_own[side] = jnp.zeros((2, total, lanes), jnp.float32)
            got_rim[side] = jnp.zeros((total, lanes), jnp.float32)

    azimuth = jnp.full(light.shape[1:], angles[0], jnp.float32)
    polar = jnp.full(light.shape[1:], angles[1], jnp.float32)
    light[0] = jnp.cos(azimuth) * jnp.sin(polar)
    light[1] = jnp.sin(azimuth) * jnp.sin(polar)
    light[2] = jnp.cos(polar)
    for c in range(4):
        line = jnp.broadcast_to(transfer[c:c + 1, :], table.shape[1:])
        table[2 * c] = line
        table[2 * c + 1] = pltpu.roll(line, lanes - 1, 1) - line

    slots = [0]
    links = {}

    def link(name, axis, step, src, dst):
        links[name, step] = (slots[0], axis, step, src, dst)
        slots[0] += 1

    def arrival(name, step):
        slot, axis, _, src, dst = links[name, -step]
        return slot, axis, src, dst

    def copy(name, step):
        slot, axis, _, src, dst = links[name, step]
        return pltpu.make_async_remote_copy(
            src_ref=src, dst_ref=dst, send_sem=send_sem.at[slot], recv_sem=recv_sem.at[slot],
            device_id=target(axis, step), device_id_type=MESH)

    def condition(name, step):
        need = has(links[name, step][1], step)
        return need

    extra = {}

    def begin(name, step):
        need = condition(name, step)
        if name in extra:
            need = jnp.logical_and(need, extra[name])
        @pl.when(need)
        def _():
            copy(name, step).start()

    def sent(name, step):
        need = condition(name, step)
        if name in extra:
            need = jnp.logical_and(need, extra[name])
        @pl.when(need)
        def _():
            copy(name, step).wait_send()

    def got(name, step):
        need = has(links[name, -step][1], step)
        if name in extra:
            need = jnp.logical_and(need, extra[name])
        @pl.when(need)
        def _():
            copy(name, -step).wait_recv()

    every = pl.ds(3, depth)
    middle = pl.ds(EDGE, rows)
    for step in (-1, 1):
        side = 0 if step > 0 else 1
        row = 0 if step < 0 else rows - EDGE
        link("rows", "gx", step, field.at[:, :, pl.ds(row, EDGE), :],
             box.at[:, every, pl.ds(EDGE + rows if step < 0 else 0, EDGE), :])
        plane = 0 if step < 0 else depth - 3
        to = depth + 3 if step < 0 else 0
        link("planes", "gz", step, field.at[:, pl.ds(plane, 3)], box.at[:, pl.ds(to, 3), middle, :])
        for name, at in (("low", 0), ("high", EDGE + rows)):
            link("planes " + name, "gz", step, box.at[:, pl.ds(3 + plane, 3), pl.ds(at, EDGE), :],
                 box.at[:, pl.ds(to, 3), pl.ds(at, EDGE), :])
        for name, at, count in (("middle", EDGE, rows), ("low", 0, EDGE), ("high", EDGE + rows, EDGE)):
            link("strips " + name, "gy", step, own_strips.at[:, pl.ds(at, count), :],
                 got_own.at[side, :, pl.ds(at, count), :])
        link("rims", "gy", step, rim_strips, got_rim.at[side])
    extra["planes low"] = has("gx", -1)
    extra["planes high"] = has("gx", 1)

    count = nz - 1
    for axis in ("gx", "gy"):
        for step in (-1, 1):
            count = count + has(axis, step).astype(jnp.int32)
    pl.semaphore_wait(barrier, count)

    for step in (-1, 1):
        begin("rows", step)
    for step in (-1, 1):
        begin("planes", step)

    lane = lax.broadcasted_iota(jnp.int32, (total, lanes), 1)

    def in_group(lane, group):
        return jnp.bitwise_and(lane + (3 + lanes) - 8 * group, lanes - 1) < 6

    def pack(at, count):
        here = lane[:count]
        def turn(z, kept):
            mask = in_group(here, z)
            return tuple(
                jnp.where(mask, pltpu.roll(box[v, 3 + z, at:at + count, :], 8 * z, 1), kept[v])
                for v in range(2))
        empty = jnp.zeros((count, lanes), jnp.float32)
        first, second = lax.fori_loop(0, depth, turn, (empty, empty))
        own_strips[0, at:at + count, :] = first
        own_strips[1, at:at + count, :] = second

    own.wait()
    pack(EDGE, rows)
    for step in (-1, 1):
        begin("strips middle", step)
    for step, name, at in ((-1, "low", 0), (1, "high", EDGE + rows)):
        got("rows", step)
        for way in (-1, 1):
            begin("planes " + name, way)
        pack(at, EDGE)
        for way in (-1, 1):
            begin("strips " + name, way)

    def merged(left, right):
        here = jnp.bitwise_and(lax.broadcasted_iota(jnp.int32, left.shape, 1), 7)
        return jnp.where(here >= 4, left, right)

    for name in ("middle", "low", "high"):
        for step in (-1, 1):
            got("strips " + name, step)
    for name in ("middle", "low", "high"):
        for step in (-1, 1):
            sent("strips " + name, step)
    for v in range(2):
        own_strips[v] = merged(got_own[0, v], got_own[1, v])

    part = 40 if total % 40 == 0 else EDGE

    def along_y(plane, group_of, strips_of):
        for at in range(0, total, part):
            here = lane[:part]
            for v in range(2):
                block = box[v, plane, at:at + part, :]
                group = group_of(v)
                halo = pltpu.roll(strips_of(v, at, part), lanes - 8 * group, 1)

                def place(o):
                    if o == 0:
                        return block
                    if o > 0:
                        return pltpu.roll(jnp.where(here < o, halo, block), lanes - o, 1)
                    return pltpu.roll(jnp.where(here >= lanes + o, halo, block), -o, 1)

                if v == 0:
                    plain, steep = both_of(place)
                    rows_done[0, plane, at:at + part, :] = plain
                    rows_done[1, plane, at:at + part, :] = steep
                else:
                    rows_done[2, plane, at:at + part, :] = smooth_of(place)

    def along_x(plane):
        width = 32 if rows % 32 == 0 else EDGE
        for at in range(0, rows, width):
            def reader(k):
                return lambda o: rows_done[k, plane, EDGE + at + o:EDGE + at + o + width, :]
            plain, steep = both_of(reader(0))
            flat_done[0, plane, at:at + width, :] = plain
            flat_done[1, plane, at:at + width, :] = steep
            flat_done[2, plane, at:at + width, :] = smooth_of(reader(1))
            flat_done[3, plane, at:at + width, :] = smooth_of(reader(2))

    def own_plane(z, carry):
        along_y(z + 3, lambda v: z, lambda v, at, count: own_strips[v, at:at + count, :])
        return carry

    def own_plane_x(z, carry):
        along_x(z + 3)
        return carry

    lax.fori_loop(0, depth, own_plane, 0)
    lax.fori_loop(0, depth, own_plane_x, 0)

    for step in (-1, 1):
        got("planes", step)
        got("planes low", step)
        got("planes high", step)

    def pack_rim(h, kept):
        plane = jnp.where(h < 3, h, h + depth)
        for v in range(2):
            group = 8 * v + h
            kept = jnp.where(in_group(lane, group), pltpu.roll(box[v, plane], 8 * group, 1), kept)
        return kept

    rim_strips[...] = lax.fori_loop(0, 6, pack_rim, jnp.zeros((total, lanes), jnp.float32))
    for step in (-1, 1):
        begin("rims", step)

    chunk = light.shape[1]

    def sample(z, at):
        def reader(k):
            return lambda o: flat_done[k, z + 3 + o, pl.ds(at, chunk), :]
        value, grad_z = both_of(reader(0))
        grad_x = smooth_of(reader(1))
        grad_y = smooth_of(reader(2))
        mixture = smooth_of(reader(3))
        position = (lanes - 1) / (1.0 + jnp.exp(-value))
        index = jnp.minimum(position.astype(jnp.int32), lanes - 2)
        share = position - index.astype(jnp.float32)

        def look(c):
            low = jnp.take_along_axis(table[2 * c], index, axis=1, mode="promise_in_bounds")
            rise = jnp.take_along_axis(table[2 * c + 1], index, axis=1, mode="promise_in_bounds")
            return low + share * rise

        facing = grad_x * light[0] + grad_y * light[1] + grad_z * light[2]
        square = grad_x * grad_x + grad_y * grad_y + grad_z * grad_z + SHADE_FLOOR
        shade = 0.25 + 0.75 * (facing * facing / square)
        alpha = 1.0 - jnp.exp((-OPTICAL * depth_step) * look(3) / (1.0 + jnp.exp(-mixture)))
        lit = alpha * shade
        return (lit * look(0), lit * look(1), lit * look(2), alpha)

    def over(front, back):
        left = 1.0 - front[3]
        return tuple(f + left * b for f, b in zip(front, back))

    nothing = tuple(jnp.zeros((chunk, lanes), jnp.float32) for _ in range(4))

    def inner_chunk(c, carry):
        at = pl.multiple_of(c * chunk, chunk)
        result = lax.fori_loop(3, depth - 3, lambda z, acc: over(acc, sample(z, at)), nothing)
        for k in range(4):
            inner[k, pl.ds(at, chunk), :] = result[k]
        return carry

    lax.fori_loop(0, rows // chunk, inner_chunk, 0)

    for step in (-1, 1):
        got("rims", step)
    for step in (-1, 1):
        sent("rims", step)
    rim_strips[...] = merged(got_rim[0], got_rim[1])

    def rim_plane(h, carry):
        plane = jnp.where(h < 3, h, h + depth)
        along_y(plane, lambda v: 8 * v + h, lambda v, at, count: rim_strips[at:at + count, :])
        return carry

    def rim_plane_x(h, carry):
        along_x(jnp.where(h < 3, h, h + depth))
        return carry

    lax.fori_loop(0, 6, rim_plane, 0)
    lax.fori_loop(0, 6, rim_plane_x, 0)

    height = rows // nz

    def slab_copy(j):
        return pltpu.make_async_remote_copy(
            src_ref=stage.at[j - 1], dst_ref=slabs.at[iz], send_sem=slab_send.at[j - 1],
            recv_sem=slab_recv.at[iz], device_id={"gz": lax.rem(iz + j, nz)}, device_id_type=MESH)

    for j in range(1, nz + 1):
        slab = lax.rem(iz + j, nz)

        def slab_chunk(c, carry):
            here = pl.multiple_of(c * chunk, chunk)
            at = pl.multiple_of(slab * height + c * chunk, chunk)
            acc = lax.fori_loop(0, 3, lambda z, a: over(a, sample(z, at)), nothing)
            acc = over(acc, tuple(inner[k, pl.ds(at, chunk), :] for k in range(4)))
            acc = lax.fori_loop(depth - 3, depth, lambda z, a: over(a, sample(z, at)), acc)
            for k in range(4):
                if j < nz:
                    stage[j - 1, k, pl.ds(here, chunk), :] = acc[k]
                else:
                    slabs[iz, k, pl.ds(here, chunk), :] = acc[k]
            return carry

        lax.fori_loop(0, height // chunk, slab_chunk, 0)
        if j < nz:
            slab_copy(j).start()

    for j in range(1, nz):
        source = lax.rem(iz + j, nz)
        pltpu.make_async_remote_copy(
            src_ref=stage.at[j - 1], dst_ref=slabs.at[source], send_sem=slab_send.at[j - 1],
            recv_sem=slab_recv.at[source], device_id={"gz": source}, device_id_type=MESH).wait_recv()

    image = tuple(slabs[0, k] for k in range(4))
    for k in range(1, nz):
        image = over(image, tuple(slabs[k, c] for c in range(4)))
    for c in range(4):
        out[c] = image[c]

    for name in ("rows", "planes", "planes low", "planes high"):
        for step in (-1, 1):
            sent(name, step)
    for j in range(1, nz):
        slab_copy(j).wait_send()


def shards(sizes, field, transfer, light_angles):
    nx, ny, nz = sizes
    _, depth, rows, lanes = field.shape
    total = rows + 2 * EDGE
    height = rows // nz
    chunk = min(height, 16)
    full = depth + 6
    f32 = jnp.float32
    return pl.pallas_call(
        functools.partial(kernel, sizes, 1.0 / (depth * nz)),
        out_shape=jax.ShapeDtypeStruct((4, height, lanes), f32),
        in_specs=[
            pl.BlockSpec(memory_space=pl.ANY),
            pl.BlockSpec(memory_space=pltpu.VMEM),
            pl.BlockSpec(memory_space=pltpu.SMEM),
        ],
        out_specs=pl.BlockSpec(memory_space=pltpu.VMEM),
        scratch_shapes=[
            pltpu.VMEM((2, full, total, lanes), f32),
            pltpu.VMEM((2, total, lanes), f32),
            pltpu.VMEM((total, lanes), f32),
            pltpu.VMEM((2, 2, total, lanes), f32),
            pltpu.VMEM((2, total, lanes), f32),
            pltpu.VMEM((3, full, total, lanes), f32),
            pltpu.VMEM((4, full, rows, lanes), f32),
            pltpu.VMEM((8, chunk, lanes), f32),
            pltpu.VMEM((3, chunk, lanes), f32),
            pltpu.VMEM((4, rows, lanes), f32),
            pltpu.VMEM((nz - 1, 4, height, lanes), f32),
            pltpu.VMEM((nz, 4, height, lanes), f32),
            pltpu.SemaphoreType.DMA,
            pltpu.SemaphoreType.DMA((16,)),
            pltpu.SemaphoreType.DMA((16,)),
            pltpu.SemaphoreType.DMA((nz,)),
            pltpu.SemaphoreType.DMA((nz,)),
        ],
        compiler_params=pltpu.CompilerParams(
            collective_id=0, has_side_effects=True, vmem_limit_bytes=40 * 1024 * 1024),
    )(field, transfer, light_angles)


def solution(mesh):
    sizes = tuple(mesh.shape[name] for name in ("gx", "gy", "gz"))
    placed = (P(None, "gz", "gx", "gy"), P(), P())
    return jax.shard_map(
        functools.partial(shards, sizes), mesh=mesh, in_specs=placed,
        out_specs=P(None, ("gx", "gz"), "gy"), check_vma=False
    )
```

```python
import functools
import math

import jax
import jax.numpy as jnp
from jax import lax
from jax.experimental import pallas as pl
from jax.experimental.pallas import tpu as pltpu
from jax.sharding import PartitionSpec as P

MESH = pl.DeviceIdType.MESH
SIGMA_TAPS = 1.2
OPTICAL = 2.0
SHADE_FLOOR = 0.25
EDGE = 8


def filter_taps():
    places = [-3, -2, -1, 0, 1, 2, 3]
    bell = [math.exp(-place * place / (2.0 * SIGMA_TAPS * SIGMA_TAPS)) for place in places]
    bell_total = sum(bell)
    slope_total = sum((place * place * weight for place, weight in zip(places, bell)))
    smooth_taps = [weight / bell_total for weight in bell]
    slope_taps = [place * weight / slope_total for place, weight in zip(places, bell)]
    return (smooth_taps, slope_taps)


def smooth_of(at):
    taps, _ = filter_taps()
    total = taps[3] * at(0)
    for o in (1, 2, 3):
        total = total + taps[3 + o] * (at(o) + at(-o))
    return total


def slope_of(at):
    _, taps = filter_taps()
    total = taps[4] * (at(1) - at(-1))
    for o in (2, 3):
        total = total + taps[3 + o] * (at(o) - at(-o))
    return total


def both_of(at):
    smooth, slope = filter_taps()
    plain, steep = smooth[3] * at(0), None
    for o in (1, 2, 3):
        after, before = at(o), at(-o)
        plain = plain + smooth[3 + o] * (after + before)
        term = slope[3 + o] * (after - before)
        steep = term if steep is None else steep + term
    return plain, steep


def kernel(sizes, depth_step, field, transfer_in, angles_in, out, transfer, angles, box, own_strips, rim_strips, got_own, got_rim,
           rows_done, flat_done, table, light, inner, stage, slabs,
           local_sem, small_sem, send_sem, recv_sem, slab_send, slab_recv):
    nx, ny, nz = sizes
    _, depth, rows, lanes = field.shape
    total = rows + 2 * EDGE
    ix, iy, iz = (lax.axis_index(name) for name in ("gx", "gy", "gz"))
    spots = {"gx": (ix, nx), "gy": (iy, ny), "gz": (iz, nz)}

    def has(axis, step):
        place, count = spots[axis]
        return place > 0 if step < 0 else place < count - 1

    def target(axis, step):
        return {axis: spots[axis][0] + step}

    barrier = pltpu.get_barrier_semaphore()
    for axis in ("gx", "gy"):
        for step in (-1, 1):
            @pl.when(has(axis, step))
            def _():
                pl.semaphore_signal(barrier, inc=1, device_id=target(axis, step), device_id_type=MESH)
    for j in range(1, nz):
        pl.semaphore_signal(barrier, inc=1, device_id={"gz": lax.rem(iz + j, nz)}, device_id_type=MESH)

    own = pltpu.make_async_copy(
        field, box.at[:, pl.ds(3, depth), pl.ds(EDGE, rows), :], local_sem)
    own.start()
    small = (pltpu.make_async_copy(transfer_in, transfer, small_sem.at[0]),
             pltpu.make_async_copy(angles_in, angles, small_sem.at[1]))
    for each in small:
        each.start()
    rim_strips[...] = jnp.zeros((rows + 2 * EDGE, lanes), jnp.float32)

    for step in (-1, 1):
        edge = 0 if step < 0 else EDGE + rows
        @pl.when(jnp.logical_not(has("gx", step)))
        def _():
            box[:, :, edge:edge + EDGE, :] = jnp.zeros((2, depth + 6, EDGE, lanes), jnp.float32)
        first = 0 if step < 0 else depth + 3
        @pl.when(jnp.logical_not(has("gz", step)))
        def _():
            flat_done[:, first:first + 3] = jnp.zeros((4, 3, rows, lanes), jnp.float32)
        side = 0 if step < 0 else 1
        @pl.when(jnp.logical_not(has("gy", step)))
        def _():
            got_own[side] = jnp.zeros((2, total, lanes), jnp.float32)
            got_rim[side] = jnp.zeros((total, lanes), jnp.float32)

    for each in small:
        each.wait()
    azimuth = jnp.full(light.shape[1:], angles[0], jnp.float32)
    polar = jnp.full(light.shape[1:], angles[1], jnp.float32)
    light[0] = jnp.cos(azimuth) * jnp.sin(polar)
    light[1] = jnp.sin(azimuth) * jnp.sin(polar)
    light[2] = jnp.cos(polar)
    for c in range(4):
        line = jnp.broadcast_to(transfer[c:c + 1, :], table.shape[1:])
        table[2 * c] = line
        table[2 * c + 1] = pltpu.roll(line, lanes - 1, 1) - line

    slots = [0]
    links = {}

    def link(name, axis, step, src, dst):
        links[name, step] = (slots[0], axis, step, src, dst)
        slots[0] += 1

    def arrival(name, step):
        slot, axis, _, src, dst = links[name, -step]
        return slot, axis, src, dst

    def copy(name, step):
        slot, axis, _, src, dst = links[name, step]
        return pltpu.make_async_remote_copy(
            src_ref=src, dst_ref=dst, send_sem=send_sem.at[slot], recv_sem=recv_sem.at[slot],
            device_id=target(axis, step), device_id_type=MESH)

    def condition(name, step):
        need = has(links[name, step][1], step)
        return need

    extra = {}

    def begin(name, step):
        need = condition(name, step)
        if name in extra:
            need = jnp.logical_and(need, extra[name])
        @pl.when(need)
        def _():
            copy(name, step).start()

    def sent(name, step):
        need = condition(name, step)
        if name in extra:
            need = jnp.logical_and(need, extra[name])
        @pl.when(need)
        def _():
            copy(name, step).wait_send()

    def got(name, step):
        need = has(links[name, -step][1], step)
        if name in extra:
            need = jnp.logical_and(need, extra[name])
        @pl.when(need)
        def _():
            copy(name, -step).wait_recv()

    every = pl.ds(3, depth)
    middle = pl.ds(EDGE, rows)
    for step in (-1, 1):
        side = 0 if step > 0 else 1
        row = 0 if step < 0 else rows - EDGE
        link("rows", "gx", step, field.at[:, :, pl.ds(row, EDGE), :],
             box.at[:, every, pl.ds(EDGE + rows if step < 0 else 0, EDGE), :])
        plane = 0 if step < 0 else depth - 3
        to = depth + 3 if step < 0 else 0
        link("planes", "gz", step, field.at[:, pl.ds(plane, 3)], box.at[:, pl.ds(to, 3), middle, :])
        for name, at in (("low", 0), ("high", EDGE + rows)):
            link("planes " + name, "gz", step, box.at[:, pl.ds(3 + plane, 3), pl.ds(at, EDGE), :],
                 box.at[:, pl.ds(to, 3), pl.ds(at, EDGE), :])
        for name, at, count in (("middle", EDGE, rows), ("low", 0, EDGE), ("high", EDGE + rows, EDGE)):
            link("strips " + name, "gy", step, own_strips.at[:, pl.ds(at, count), :],
                 got_own.at[side, :, pl.ds(at, count), :])
        link("rims", "gy", step, rim_strips, got_rim.at[side])
    extra["planes low"] = has("gx", -1)
    extra["planes high"] = has("gx", 1)

    count = nz - 1
    for axis in ("gx", "gy"):
        for step in (-1, 1):
            count = count + has(axis, step).astype(jnp.int32)
    pl.semaphore_wait(barrier, count)

    for step in (-1, 1):
        begin("rows", step)
    for step in (-1, 1):
        begin("planes", step)

    lane = lax.broadcasted_iota(jnp.int32, (total, lanes), 1)

    def in_group(lane, group):
        return jnp.bitwise_and(lane + (3 + lanes) - 8 * group, lanes - 1) < 6

    def pack(at, count):
        here = lane[:count]
        def turn(z, kept):
            mask = in_group(here, z)
            return tuple(
                jnp.where(mask, pltpu.roll(box[v, 3 + z, at:at + count, :], 8 * z, 1), kept[v])
                for v in range(2))
        empty = jnp.zeros((count, lanes), jnp.float32)
        first, second = lax.fori_loop(0, depth, turn, (empty, empty))
        own_strips[0, at:at + count, :] = first
        own_strips[1, at:at + count, :] = second

    own.wait()
    pack(EDGE, rows)
    for step in (-1, 1):
        begin("strips middle", step)
    for step, name, at in ((-1, "low", 0), (1, "high", EDGE + rows)):
        got("rows", step)
        for way in (-1, 1):
            begin("planes " + name, way)
        pack(at, EDGE)
        for way in (-1, 1):
            begin("strips " + name, way)

    def merged(left, right):
        here = jnp.bitwise_and(lax.broadcasted_iota(jnp.int32, left.shape, 1), 7)
        return jnp.where(here >= 4, left, right)

    def unite(at, count):
        for v in range(2):
            own_strips[v, at:at + count, :] = merged(
                got_own[0, v, at:at + count, :], got_own[1, v, at:at + count, :])

    def along_y(v, plane, at, count, group, strips):
        here = lane[:count]
        block = box[v, plane, at:at + count, :]
        halo = pltpu.roll(strips, lanes - 8 * group, 1)

        def place(o):
            if o == 0:
                return block
            if o > 0:
                return pltpu.roll(jnp.where(here < o, halo, block), lanes - o, 1)
            return pltpu.roll(jnp.where(here >= lanes + o, halo, block), -o, 1)

        return both_of(place) if v == 0 else (smooth_of(place),)

    def own_y(blocks, planes):
        def turn(i, carry):
            done = []
            for p in range(planes):
                z = i * planes + p
                for at, count in blocks:
                    found = []
                    for v in range(2):
                        found += along_y(v, z + 3, at, count, z, own_strips[v, at:at + count, :])
                    done.append((z + 3, at, count, found))
            for plane, at, count, found in done:
                for k in range(3):
                    rows_done[k, plane, at:at + count, :] = found[k]
            return carry
        lax.fori_loop(0, depth // planes, turn, 0)

    def along_x(plane):
        width = 32 if rows % 32 == 0 else EDGE
        for at in range(0, rows, width):
            def reader(k):
                return lambda o: rows_done[k, plane, EDGE + at + o:EDGE + at + o + width, :]
            plain, steep = both_of(reader(0))
            crossed, other = smooth_of(reader(1)), smooth_of(reader(2))
            for k, found in enumerate((plain, steep, crossed, other)):
                flat_done[k, plane, at:at + width, :] = found

    def own_x(z, carry):
        along_x(z + 3)
        return carry

    for step in (-1, 1):
        got("strips middle", step)
    for step in (-1, 1):
        sent("strips middle", step)
    unite(EDGE, rows)
    own_y([(at, 32) for at in range(EDGE, EDGE + rows, 32)], 1)
    for name in ("low", "high"):
        for step in (-1, 1):
            got("strips " + name, step)
    for name in ("low", "high"):
        for step in (-1, 1):
            sent("strips " + name, step)
    unite(0, EDGE)
    unite(EDGE + rows, EDGE)
    own_y([(0, EDGE), (EDGE + rows, EDGE)], 4)
    lax.fori_loop(0, depth, own_x, 0)

    for step in (-1, 1):
        got("planes", step)
        got("planes low", step)
        got("planes high", step)

    rims = {-1: ((0, 0), (1, 1), (2, 2)), 1: tuple((3 + h, depth + 3 + h) for h in range(3))}
    for step in (-1, 1):
        @pl.when(has("gz", step))
        def _():
            kept = rim_strips[...]
            for h, plane in rims[step]:
                for v in range(2):
                    group = 8 * v + h
                    kept = jnp.where(in_group(lane, group), pltpu.roll(box[v, plane], 8 * group, 1), kept)
            rim_strips[...] = kept

    for step in (-1, 1):
        begin("rims", step)

    def sample(z, at, chunk):
        def reader(k):
            return lambda o: flat_done[k, z + 3 + o, pl.ds(at, chunk), :]
        value, grad_z = both_of(reader(0))
        grad_x = smooth_of(reader(1))
        grad_y = smooth_of(reader(2))
        mixture = smooth_of(reader(3))
        position = (lanes - 1) / (1.0 + jnp.exp(-value))
        index = jnp.minimum(position.astype(jnp.int32), lanes - 2)
        share = position - index.astype(jnp.float32)

        def look(c):
            low = jnp.take_along_axis(table[2 * c, :chunk], index, axis=1, mode="promise_in_bounds")
            rise = jnp.take_along_axis(table[2 * c + 1, :chunk], index, axis=1, mode="promise_in_bounds")
            return low + share * rise

        facing = grad_x * light[0, :chunk] + grad_y * light[1, :chunk] + grad_z * light[2, :chunk]
        square = grad_x * grad_x + grad_y * grad_y + grad_z * grad_z + SHADE_FLOOR
        shade = 0.25 + 0.75 * (facing * facing / square)
        alpha = 1.0 - jnp.exp((-OPTICAL * depth_step) * look(3) / (1.0 + jnp.exp(-mixture)))
        lit = alpha * shade
        return (lit * look(0), lit * look(1), lit * look(2), alpha)

    def over(front, back):
        left = 1.0 - front[3]
        return tuple(f + left * b for f, b in zip(front, back))

    def nothing(chunk):
        return tuple(jnp.zeros((chunk, lanes), jnp.float32) for _ in range(4))

    wide = light.shape[1]

    def inner_chunk(c, carry):
        at = pl.multiple_of(c * wide, wide)

        def turn(i, acc):
            z = 3 + 2 * i
            pair = [sample(z + p, at, wide) for p in range(2)]
            return over(acc, over(*pair))

        result = lax.fori_loop(0, (depth - 6) // 2, turn, nothing(wide))
        for k in range(4):
            inner[k, pl.ds(at, wide), :] = result[k]
        return carry

    lax.fori_loop(0, rows // wide, inner_chunk, 0)

    for step in (-1, 1):
        got("rims", step)
    for step in (-1, 1):
        sent("rims", step)
    rim_strips[...] = merged(got_rim[0], got_rim[1])

    for step in (-1, 1):
        @pl.when(has("gz", step))
        def _():
            for h, plane in rims[step]:
                for at in range(0, total, 40):
                    found = []
                    for v in range(2):
                        found += along_y(v, plane, at, 40, 8 * v + h, rim_strips[at:at + 40, :])
                    for k in range(3):
                        rows_done[k, plane, at:at + 40, :] = found[k]
            for h, plane in rims[step]:
                along_x(plane)

    height = rows // nz

    def slab_copy(j):
        return pltpu.make_async_remote_copy(
            src_ref=stage.at[j - 1], dst_ref=slabs.at[iz], send_sem=slab_send.at[j - 1],
            recv_sem=slab_recv.at[iz], device_id={"gz": lax.rem(iz + j, nz)}, device_id_type=MESH)

    for j in range(1, nz + 1):
        slab = lax.rem(iz + j, nz)

        at = pl.multiple_of(slab * height, height)
        acc = sample(0, at, height)
        for z in (1, 2):
            acc = over(acc, sample(z, at, height))
        acc = over(acc, tuple(inner[k, pl.ds(at, height), :] for k in range(4)))
        for z in range(depth - 3, depth):
            acc = over(acc, sample(z, at, height))
        for k in range(4):
            if j < nz:
                stage[j - 1, k] = acc[k]
            else:
                slabs[iz, k] = acc[k]
        if j < nz:
            slab_copy(j).start()

    for j in range(1, nz):
        source = lax.rem(iz + j, nz)
        pltpu.make_async_remote_copy(
            src_ref=stage.at[j - 1], dst_ref=slabs.at[source], send_sem=slab_send.at[j - 1],
            recv_sem=slab_recv.at[source], device_id={"gz": source}, device_id_type=MESH).wait_recv()

    image = tuple(slabs[0, k] for k in range(4))
    for k in range(1, nz):
        image = over(image, tuple(slabs[k, c] for c in range(4)))
    for c in range(4):
        out[c] = image[c]

    for name in ("rows", "planes", "planes low", "planes high"):
        for step in (-1, 1):
            sent(name, step)
    for j in range(1, nz):
        slab_copy(j).wait_send()


def shards(sizes, field, transfer, light_angles):
    nx, ny, nz = sizes
    _, depth, rows, lanes = field.shape
    total = rows + 2 * EDGE
    height = rows // nz
    chunk = 32
    full = depth + 6
    f32 = jnp.float32
    return pl.pallas_call(
        functools.partial(kernel, sizes, 1.0 / (depth * nz)),
        out_shape=jax.ShapeDtypeStruct((4, height, lanes), f32),
        in_specs=[
            pl.BlockSpec(memory_space=pl.ANY),
            pl.BlockSpec(memory_space=pl.ANY),
            pl.BlockSpec(memory_space=pl.ANY),
        ],
        out_specs=pl.BlockSpec(memory_space=pltpu.VMEM),
        scratch_shapes=[
            pltpu.VMEM((4, lanes), f32),
            pltpu.SMEM((2,), f32),
            pltpu.VMEM((2, full, total, lanes), f32),
            pltpu.VMEM((2, total, lanes), f32),
            pltpu.VMEM((total, lanes), f32),
            pltpu.VMEM((2, 2, total, lanes), f32),
            pltpu.VMEM((2, total, lanes), f32),
            pltpu.VMEM((3, full, total, lanes), f32),
            pltpu.VMEM((4, full, rows, lanes), f32),
            pltpu.VMEM((8, chunk, lanes), f32),
            pltpu.VMEM((3, chunk, lanes), f32),
            pltpu.VMEM((4, rows, lanes), f32),
            pltpu.VMEM((nz - 1, 4, height, lanes), f32),
            pltpu.VMEM((nz, 4, height, lanes), f32),
            pltpu.SemaphoreType.DMA,
            pltpu.SemaphoreType.DMA((2,)),
            pltpu.SemaphoreType.DMA((16,)),
            pltpu.SemaphoreType.DMA((16,)),
            pltpu.SemaphoreType.DMA((nz,)),
            pltpu.SemaphoreType.DMA((nz,)),
        ],
        compiler_params=pltpu.CompilerParams(
            collective_id=0, has_side_effects=True, vmem_limit_bytes=62 * 1024 * 1024),
    )(field, transfer, light_angles)


def solution(mesh):
    sizes = tuple(mesh.shape[name] for name in ("gx", "gy", "gz"))
    placed = (P(None, "gz", "gx", "gy"), P(), P())
    return jax.shard_map(
        functools.partial(shards, sizes), mesh=mesh, in_specs=placed,
        out_specs=P(None, ("gx", "gz"), "gy"), check_vma=False
    )
```

```python
import functools
import math

import jax
import jax.numpy as jnp
from jax import lax
from jax.experimental import pallas as pl
from jax.experimental.pallas import tpu as pltpu
from jax.sharding import PartitionSpec as P

MESH = pl.DeviceIdType.MESH
SIGMA_TAPS = 1.2
OPTICAL = 2.0
SHADE_FLOOR = 0.25
EDGE = 8


def filter_taps():
    places = [-3, -2, -1, 0, 1, 2, 3]
    bell = [math.exp(-place * place / (2.0 * SIGMA_TAPS * SIGMA_TAPS)) for place in places]
    bell_total = sum(bell)
    slope_total = sum((place * place * weight for place, weight in zip(places, bell)))
    smooth_taps = [weight / bell_total for weight in bell]
    slope_taps = [place * weight / slope_total for place, weight in zip(places, bell)]
    return (smooth_taps, slope_taps)


def smooth_of(at):
    taps, _ = filter_taps()
    total = taps[3] * at(0)
    for o in (1, 2, 3):
        total = total + taps[3 + o] * (at(o) + at(-o))
    return total


def slope_of(at):
    _, taps = filter_taps()
    total = taps[4] * (at(1) - at(-1))
    for o in (2, 3):
        total = total + taps[3 + o] * (at(o) - at(-o))
    return total


def both_of(at):
    smooth, slope = filter_taps()
    plain, steep = smooth[3] * at(0), None
    for o in (1, 2, 3):
        after, before = at(o), at(-o)
        plain = plain + smooth[3 + o] * (after + before)
        term = slope[3 + o] * (after - before)
        steep = term if steep is None else steep + term
    return plain, steep


def kernel(sizes, depth_step, field, transfer_in, angles_in, out, transfer, angles, box, own_strips, rim_strips, got_own, got_rim, joined,
           rows_done, flat_done, table, light, inner, stage, slabs,
           local_sem, small_sem, send_sem, recv_sem, slab_send, slab_recv):
    nx, ny, nz = sizes
    _, depth, rows, lanes = field.shape
    total = rows + 2 * EDGE
    ix, iy, iz = (lax.axis_index(name) for name in ("gx", "gy", "gz"))
    spots = (("gx", ix, nx), ("gy", iy, ny), ("gz", iz, nz))

    def has(way):
        need = None
        for (_, place, count), step in zip(spots, way):
            if step:
                here = place > 0 if step < 0 else place < count - 1
                need = here if need is None else jnp.logical_and(need, here)
        return need

    def target(way):
        return {name: place + step for (name, place, _), step in zip(spots, way) if step}

    def lies(axis, step):
        return tuple(step if k == axis else 0 for k in range(3))

    flat_ways = [(dx, dy, 0) for dx in (-1, 0, 1) for dy in (-1, 0, 1) if dx or dy]
    sides = (-1, 1)

    barrier = pltpu.get_barrier_semaphore()
    for way in flat_ways:
        @pl.when(has(way))
        def _():
            pl.semaphore_signal(barrier, inc=1, device_id=target(way), device_id_type=MESH)
    for j in range(1, nz):
        pl.semaphore_signal(barrier, inc=1, device_id={"gz": lax.rem(iz + j, nz)}, device_id_type=MESH)

    own = pltpu.make_async_copy(
        field, box.at[:, pl.ds(3, depth), pl.ds(EDGE, rows), :], local_sem)
    own.start()
    small = (pltpu.make_async_copy(transfer_in, transfer, small_sem.at[0]),
             pltpu.make_async_copy(angles_in, angles, small_sem.at[1]))
    for each in small:
        each.start()
    rim_strips[...] = jnp.zeros((rows + 2 * EDGE, lanes), jnp.float32)

    for step in sides:
        edge = 0 if step < 0 else EDGE + rows
        @pl.when(jnp.logical_not(has(lies(0, step))))
        def _():
            box[:, :, edge:edge + EDGE, :] = jnp.zeros((2, depth + 6, EDGE, lanes), jnp.float32)
            got_own[:, :, edge:edge + EDGE, :] = jnp.zeros((2, 2, EDGE, lanes), jnp.float32)
        first = 0 if step < 0 else depth + 3
        @pl.when(jnp.logical_not(has(lies(2, step))))
        def _():
            flat_done[:, first:first + 3] = jnp.zeros((4, 3, rows, lanes), jnp.float32)
        side = 0 if step < 0 else 1
        @pl.when(jnp.logical_not(has(lies(1, step))))
        def _():
            got_own[side] = jnp.zeros((2, total, lanes), jnp.float32)
            got_rim[side] = jnp.zeros((total, lanes), jnp.float32)

    for each in small:
        each.wait()
    azimuth = jnp.full(light.shape[1:], angles[0], jnp.float32)
    polar = jnp.full(light.shape[1:], angles[1], jnp.float32)
    light[0] = jnp.cos(azimuth) * jnp.sin(polar)
    light[1] = jnp.sin(azimuth) * jnp.sin(polar)
    light[2] = jnp.cos(polar)
    for c in range(4):
        line = jnp.broadcast_to(transfer[c:c + 1, :], table.shape[1:])
        table[2 * c] = line
        table[2 * c + 1] = pltpu.roll(line, lanes - 1, 1) - line

    links = {}

    def link(name, way, src, dst, need=None):
        links[name, way] = (len(links), src, dst, need)

    def wanted(name, way):
        need, more = has(way), links[name, way][3]
        return need if more is None else jnp.logical_and(need, more)

    def copy(name, way):
        slot, src, dst, _ = links[name, way]
        return pltpu.make_async_remote_copy(
            src_ref=src, dst_ref=dst, send_sem=send_sem.at[slot], recv_sem=recv_sem.at[slot],
            device_id=target(way), device_id_type=MESH)

    def begin(name, way):
        @pl.when(wanted(name, way))
        def _():
            copy(name, way).start()

    def sent(name, way):
        @pl.when(wanted(name, way))
        def _():
            copy(name, way).wait_send()

    def got(name, way):
        back = tuple(-step for step in way)
        need, more = has(way), links[name, back][3]
        @pl.when(need if more is None else jnp.logical_and(need, more))
        def _():
            copy(name, back).wait_recv()

    every = pl.ds(3, depth)
    middle = pl.ds(EDGE, rows)

    def rows_from(dx):
        return middle if dx == 0 else pl.ds(EDGE if dx < 0 else rows, EDGE)

    def rows_to(dx):
        return middle if dx == 0 else pl.ds(EDGE + rows if dx < 0 else 0, EDGE)

    for way in flat_ways:
        if way[1]:
            side = 0 if way[1] > 0 else 1
            link("strips", way, own_strips.at[:, rows_from(way[0]), :], got_own.at[side, :, rows_to(way[0]), :])
    for step in sides:
        row = 0 if step < 0 else rows - EDGE
        link("rows", lies(0, step), field.at[:, :, pl.ds(row, EDGE), :], box.at[:, every, rows_to(step), :])
        plane = 0 if step < 0 else depth - 3
        to = depth + 3 if step < 0 else 0
        link("planes", lies(2, step), field.at[:, pl.ds(plane, 3)], box.at[:, pl.ds(to, 3), middle, :])
        for name, at, side in (("low", 0, -1), ("high", EDGE + rows, 1)):
            link(name, lies(2, step), box.at[:, pl.ds(3 + plane, 3), pl.ds(at, EDGE), :],
                 box.at[:, pl.ds(to, 3), pl.ds(at, EDGE), :], has(lies(0, side)))
        link("rims", lies(1, step), rim_strips, got_rim.at[0 if step > 0 else 1])

    count = nz - 1
    for way in flat_ways:
        count = count + has(way).astype(jnp.int32)

    lane = lax.broadcasted_iota(jnp.int32, (total, lanes), 1)

    def in_group(lane, group):
        return jnp.bitwise_and(lane + (3 + lanes) - 8 * group, lanes - 1) < 6

    own.wait()

    def pack(z, kept):
        mask = in_group(lane[:rows], z)
        return tuple(
            jnp.where(mask, pltpu.roll(box[v, 3 + z, EDGE:EDGE + rows, :], 8 * z, 1), kept[v])
            for v in range(2))

    empty = jnp.zeros((rows, lanes), jnp.float32)
    packed = lax.fori_loop(0, depth, pack, (empty, empty))
    for v in range(2):
        own_strips[v, EDGE:EDGE + rows, :] = packed[v]

    pl.semaphore_wait(barrier, count)
    strip_ways = [way for way in flat_ways if way[1]]
    for way in strip_ways:
        begin("strips", way)
    for step in sides:
        begin("rows", lies(0, step))
    for step in sides:
        begin("planes", lies(2, step))

    def merged(left, right):
        here = jnp.bitwise_and(lax.broadcasted_iota(jnp.int32, left.shape, 1), 7)
        return jnp.where(here >= 4, left, right)

    def along_y(v, plane, at, count, group, strips):
        here = lane[:count]
        block = box[v, plane, at:at + count, :]
        halo = pltpu.roll(strips, lanes - 8 * group, 1)

        def place(o):
            if o == 0:
                return block
            if o > 0:
                return pltpu.roll(jnp.where(here < o, halo, block), lanes - o, 1)
            return pltpu.roll(jnp.where(here >= lanes + o, halo, block), -o, 1)

        return both_of(place) if v == 0 else (smooth_of(place),)

    def own_y(blocks, planes):
        def turn(i, carry):
            done = []
            for p in range(planes):
                z = i * planes + p
                for at, count in blocks:
                    found = []
                    for v in range(2):
                        found += along_y(v, z + 3, at, count, z, joined[v, at:at + count, :])
                    done.append((z + 3, at, count, found))
            for plane, at, count, found in done:
                for k in range(3):
                    rows_done[k, plane, at:at + count, :] = found[k]
            return carry
        lax.fori_loop(0, depth // planes, turn, 0)

    def along_x(plane):
        width = 32 if rows % 32 == 0 else EDGE
        for at in range(0, rows, width):
            def reader(k):
                return lambda o: rows_done[k, plane, EDGE + at + o:EDGE + at + o + width, :]
            plain, steep = both_of(reader(0))
            crossed, other = smooth_of(reader(1)), smooth_of(reader(2))
            for k, found in enumerate((plain, steep, crossed, other)):
                flat_done[k, plane, at:at + width, :] = found

    def own_x(z, carry):
        along_x(z + 3)
        return carry

    for step, name in ((-1, "low"), (1, "high")):
        got("rows", lies(0, step))
        for side in sides:
            begin(name, lies(2, side))
    for way in strip_ways:
        got("strips", way)
    for v in range(2):
        joined[v] = merged(got_own[0, v], got_own[1, v])
    own_y([(at, 40) for at in range(0, total, 40)], 1)
    lax.fori_loop(0, depth, own_x, 0)

    for step in sides:
        for name in ("planes", "low", "high"):
            got(name, lies(2, step))

    rims = {-1: ((0, 0), (1, 1), (2, 2)), 1: tuple((3 + h, depth + 3 + h) for h in range(3))}
    for step in sides:
        @pl.when(has(lies(2, step)))
        def _():
            kept = rim_strips[...]
            for h, plane in rims[step]:
                for v in range(2):
                    group = 8 * v + h
                    kept = jnp.where(in_group(lane, group), pltpu.roll(box[v, plane], 8 * group, 1), kept)
            rim_strips[...] = kept

    for step in sides:
        begin("rims", lies(1, step))

    def sample(z, at, chunk):
        def reader(k):
            return lambda o: flat_done[k, z + 3 + o, pl.ds(at, chunk), :]
        value, grad_z = both_of(reader(0))
        grad_x = smooth_of(reader(1))
        grad_y = smooth_of(reader(2))
        mixture = smooth_of(reader(3))
        position = (lanes - 1) / (1.0 + jnp.exp(-value))
        index = jnp.minimum(position.astype(jnp.int32), lanes - 2)
        share = position - index.astype(jnp.float32)

        def look(c):
            low = jnp.take_along_axis(table[2 * c, :chunk], index, axis=1, mode="promise_in_bounds")
            rise = jnp.take_along_axis(table[2 * c + 1, :chunk], index, axis=1, mode="promise_in_bounds")
            return low + share * rise

        facing = grad_x * light[0, :chunk] + grad_y * light[1, :chunk] + grad_z * light[2, :chunk]
        square = grad_x * grad_x + grad_y * grad_y + grad_z * grad_z + SHADE_FLOOR
        shade = 0.25 + 0.75 * (facing * facing / square)
        alpha = 1.0 - jnp.exp((-OPTICAL * depth_step) * look(3) / (1.0 + jnp.exp(-mixture)))
        lit = alpha * shade
        return (lit * look(0), lit * look(1), lit * look(2), alpha)

    def over(front, back):
        left = 1.0 - front[3]
        return tuple(f + left * b for f, b in zip(front, back))

    def nothing(chunk):
        return tuple(jnp.zeros((chunk, lanes), jnp.float32) for _ in range(4))

    wide = light.shape[1]

    height = rows // nz
    inner_rows = min(height, wide)

    def inner_slab(slab):
        def inner_chunk(c, carry):
            at = pl.multiple_of(slab * height + c * inner_rows, inner_rows)

            def turn(i, acc):
                z = 3 + 2 * i
                pair = [sample(z + p, at, inner_rows) for p in range(2)]
                return over(acc, over(*pair))

            result = lax.fori_loop(0, (depth - 6) // 2, turn, nothing(inner_rows))
            for k in range(4):
                inner[k, pl.ds(at, inner_rows), :] = result[k]
            return carry

        lax.fori_loop(0, height // inner_rows, inner_chunk, 0)

    for j in range(1, nz):
        inner_slab(lax.rem(iz + j, nz))

    for step in sides:
        got("rims", lies(1, step))
    joined[0] = merged(got_rim[0], got_rim[1])

    for step in sides:
        @pl.when(has(lies(2, step)))
        def _():
            for h, plane in rims[step]:
                for at in range(0, total, 40):
                    found = []
                    for v in range(2):
                        found += along_y(v, plane, at, 40, 8 * v + h, joined[0, at:at + 40, :])
                    for k in range(3):
                        rows_done[k, plane, at:at + 40, :] = found[k]
            for h, plane in rims[step]:
                along_x(plane)

    def slab_copy(j):
        return pltpu.make_async_remote_copy(
            src_ref=stage.at[j - 1], dst_ref=slabs.at[iz], send_sem=slab_send.at[j - 1],
            recv_sem=slab_recv.at[iz], device_id={"gz": lax.rem(iz + j, nz)}, device_id_type=MESH)

    for j in range(1, nz + 1):
        slab = lax.rem(iz + j, nz)
        if j == nz:
            inner_slab(slab)

        at = pl.multiple_of(slab * height, height)
        acc = sample(0, at, height)
        for z in (1, 2):
            acc = over(acc, sample(z, at, height))
        acc = over(acc, tuple(inner[k, pl.ds(at, height), :] for k in range(4)))
        for z in range(depth - 3, depth):
            acc = over(acc, sample(z, at, height))
        for k in range(4):
            if j < nz:
                stage[j - 1, k] = acc[k]
            else:
                slabs[iz, k] = acc[k]
        if j < nz:
            slab_copy(j).start()

    for j in range(1, nz):
        source = lax.rem(iz + j, nz)
        pltpu.make_async_remote_copy(
            src_ref=stage.at[j - 1], dst_ref=slabs.at[source], send_sem=slab_send.at[j - 1],
            recv_sem=slab_recv.at[source], device_id={"gz": source}, device_id_type=MESH).wait_recv()

    image = tuple(slabs[0, k] for k in range(4))
    for k in range(1, nz):
        image = over(image, tuple(slabs[k, c] for c in range(4)))
    for c in range(4):
        out[c] = image[c]

    for name, way in links:
        sent(name, way)
    for j in range(1, nz):
        slab_copy(j).wait_send()


def shards(sizes, field, transfer, light_angles):
    nx, ny, nz = sizes
    _, depth, rows, lanes = field.shape
    total = rows + 2 * EDGE
    height = rows // nz
    chunk = 32
    full = depth + 6
    f32 = jnp.float32
    return pl.pallas_call(
        functools.partial(kernel, sizes, 1.0 / (depth * nz)),
        out_shape=jax.ShapeDtypeStruct((4, height, lanes), f32),
        in_specs=[
            pl.BlockSpec(memory_space=pltpu.HBM),
            pl.BlockSpec(memory_space=pltpu.HBM),
            pl.BlockSpec(memory_space=pltpu.HBM),
        ],
        out_specs=pl.BlockSpec(memory_space=pltpu.VMEM),
        scratch_shapes=[
            pltpu.VMEM((4, lanes), f32),
            pltpu.SMEM((2,), f32),
            pltpu.VMEM((2, full, total, lanes), f32),
            pltpu.VMEM((2, total, lanes), f32),
            pltpu.VMEM((total, lanes), f32),
            pltpu.VMEM((2, 2, total, lanes), f32),
            pltpu.VMEM((2, total, lanes), f32),
            pltpu.VMEM((2, total, lanes), f32),
            pltpu.VMEM((3, full, total, lanes), f32),
            pltpu.VMEM((4, full, rows, lanes), f32),
            pltpu.VMEM((8, chunk, lanes), f32),
            pltpu.VMEM((3, chunk, lanes), f32),
            pltpu.VMEM((4, rows, lanes), f32),
            pltpu.VMEM((nz - 1, 4, height, lanes), f32),
            pltpu.VMEM((nz, 4, height, lanes), f32),
            pltpu.SemaphoreType.DMA,
            pltpu.SemaphoreType.DMA((2,)),
            pltpu.SemaphoreType.DMA((20,)),
            pltpu.SemaphoreType.DMA((20,)),
            pltpu.SemaphoreType.DMA((nz,)),
            pltpu.SemaphoreType.DMA((nz,)),
        ],
        compiler_params=pltpu.CompilerParams(
            collective_id=0, has_side_effects=True, vmem_limit_bytes=40 * 1024 * 1024),
    )(*(pltpu.with_memory_space_constraint(x, pltpu.HBM) for x in (field, transfer, light_angles)))


def solution(mesh):
    sizes = tuple(mesh.shape[name] for name in ("gx", "gy", "gz"))
    placed = (P(None, "gz", "gx", "gy"), P(), P())
    return jax.shard_map(
        functools.partial(shards, sizes), mesh=mesh, in_specs=placed,
        out_specs=P(None, ("gx", "gz"), "gy"), check_vma=False
    )
```

```python
import functools
import math

import jax
import jax.numpy as jnp
from jax import lax
from jax.experimental import pallas as pl
from jax.experimental.pallas import tpu as pltpu
from jax.sharding import PartitionSpec as P

MESH = pl.DeviceIdType.MESH
SIGMA_TAPS = 1.2
OPTICAL = 2.0
SHADE_FLOOR = 0.25
EDGE = 8


def filter_taps():
    places = [-3, -2, -1, 0, 1, 2, 3]
    bell = [math.exp(-place * place / (2.0 * SIGMA_TAPS * SIGMA_TAPS)) for place in places]
    bell_total = sum(bell)
    slope_total = sum((place * place * weight for place, weight in zip(places, bell)))
    smooth_taps = [weight / bell_total for weight in bell]
    slope_taps = [place * weight / slope_total for place, weight in zip(places, bell)]
    return (smooth_taps, slope_taps)


def smooth_of(at):
    taps, _ = filter_taps()
    total = taps[3] * at(0)
    for o in (1, 2, 3):
        total = total + taps[3 + o] * (at(o) + at(-o))
    return total


def slope_of(at):
    _, taps = filter_taps()
    total = taps[4] * (at(1) - at(-1))
    for o in (2, 3):
        total = total + taps[3 + o] * (at(o) - at(-o))
    return total


def both_of(at):
    smooth, slope = filter_taps()
    plain, steep = smooth[3] * at(0), None
    for o in (1, 2, 3):
        after, before = at(o), at(-o)
        plain = plain + smooth[3 + o] * (after + before)
        term = slope[3 + o] * (after - before)
        steep = term if steep is None else steep + term
    return plain, steep


def kernel(sizes, depth_step, field, transfer_in, angles_in, out, transfer, angles, box, own_strips, rim_strips, got_own, got_rim, joined,
           rows_done, flat_done, table, light, inner, stage, slabs,
           local_sem, small_sem, send_sem, recv_sem, slab_send, slab_recv):
    nx, ny, nz = sizes
    _, depth, rows, lanes = field.shape
    total = rows + 2 * EDGE
    ix, iy, iz = (lax.axis_index(name) for name in ("gx", "gy", "gz"))
    spots = (("gx", ix, nx), ("gy", iy, ny), ("gz", iz, nz))

    def has(way):
        need = None
        for (_, place, count), step in zip(spots, way):
            if step:
                here = place > 0 if step < 0 else place < count - 1
                need = here if need is None else jnp.logical_and(need, here)
        return need

    def target(way):
        return {name: place + step for (name, place, _), step in zip(spots, way) if step}

    def lies(axis, step):
        return tuple(step if k == axis else 0 for k in range(3))

    flat_ways = [(dx, dy, 0) for dx in (-1, 0, 1) for dy in (-1, 0, 1) if dx or dy]
    sides = (-1, 1)

    barrier = pltpu.get_barrier_semaphore()
    for way in flat_ways:
        @pl.when(has(way))
        def _():
            pl.semaphore_signal(barrier, inc=1, device_id=target(way), device_id_type=MESH)
    for j in range(1, nz):
        pl.semaphore_signal(barrier, inc=1, device_id={"gz": lax.rem(iz + j, nz)}, device_id_type=MESH)

    own = pltpu.make_async_copy(
        field, box.at[:, pl.ds(3, depth), pl.ds(EDGE, rows), :], local_sem)
    own.start()
    small = (pltpu.make_async_copy(transfer_in, transfer, small_sem.at[0]),
             pltpu.make_async_copy(angles_in, angles, small_sem.at[1]))
    for each in small:
        each.start()

    for step in sides:
        edge = 0 if step < 0 else EDGE + rows
        @pl.when(jnp.logical_not(has(lies(0, step))))
        def _():
            box[:, :, edge:edge + EDGE, :] = jnp.zeros((2, depth + 6, EDGE, lanes), jnp.float32)
            got_own[:, :, edge:edge + EDGE, :] = jnp.zeros((2, 2, EDGE, lanes), jnp.float32)
        first = 0 if step < 0 else depth + 3
        @pl.when(jnp.logical_not(has(lies(2, step))))
        def _():
            flat_done[:, first:first + 3] = jnp.zeros((4, 3, rows, lanes), jnp.float32)
        side = 0 if step < 0 else 1
        @pl.when(jnp.logical_not(has(lies(1, step))))
        def _():
            got_own[side] = jnp.zeros((2, total, lanes), jnp.float32)

    for each in small:
        each.wait()
    azimuth = jnp.full(light.shape[1:], angles[0], jnp.float32)
    polar = jnp.full(light.shape[1:], angles[1], jnp.float32)
    light[0] = jnp.cos(azimuth) * jnp.sin(polar)
    light[1] = jnp.sin(azimuth) * jnp.sin(polar)
    light[2] = jnp.cos(polar)
    for c in range(4):
        line = jnp.broadcast_to(transfer[c:c + 1, :], table.shape[1:])
        table[2 * c] = line
        table[2 * c + 1] = pltpu.roll(line, lanes - 1, 1) - line

    links = {}

    def link(name, way, src, dst, need=None):
        links[name, way] = (len(links), src, dst, need)

    def wanted(name, way):
        need, more = has(way), links[name, way][3]
        return need if more is None else jnp.logical_and(need, more)

    def copy(name, way):
        slot, src, dst, _ = links[name, way]
        return pltpu.make_async_remote_copy(
            src_ref=src, dst_ref=dst, send_sem=send_sem.at[slot], recv_sem=recv_sem.at[slot],
            device_id=target(way), device_id_type=MESH)

    def begin(name, way):
        @pl.when(wanted(name, way))
        def _():
            copy(name, way).start()

    def sent(name, way):
        @pl.when(wanted(name, way))
        def _():
            copy(name, way).wait_send()

    def got(name, way):
        back = tuple(-step for step in way)
        need, more = has(way), links[name, back][3]
        @pl.when(need if more is None else jnp.logical_and(need, more))
        def _():
            copy(name, back).wait_recv()

    every = pl.ds(3, depth)
    middle = pl.ds(EDGE, rows)

    def rows_from(dx):
        return middle if dx == 0 else pl.ds(EDGE if dx < 0 else rows, EDGE)

    def rows_to(dx):
        return middle if dx == 0 else pl.ds(EDGE + rows if dx < 0 else 0, EDGE)

    for way in flat_ways:
        if way[1]:
            side = 0 if way[1] > 0 else 1
            link("strips", way, own_strips.at[:, rows_from(way[0]), :], got_own.at[side, :, rows_to(way[0]), :])
    for step in sides:
        row = 0 if step < 0 else rows - EDGE
        link("rows", lies(0, step), field.at[:, :, pl.ds(row, EDGE), :], box.at[:, every, rows_to(step), :])
        plane = 0 if step < 0 else depth - 3
        to = depth + 3 if step < 0 else 0
        link("planes", lies(2, step), field.at[:, pl.ds(plane, 3)], box.at[:, pl.ds(to, 3), middle, :])
        for name, at, side in (("low", 0, -1), ("high", EDGE + rows, 1)):
            link(name, lies(2, step), box.at[:, pl.ds(3 + plane, 3), pl.ds(at, EDGE), :],
                 box.at[:, pl.ds(to, 3), pl.ds(at, EDGE), :], has(lies(0, side)))
        link("rims", lies(2, step), rim_strips.at[0 if step < 0 else 1], got_rim.at[0 if step > 0 else 1])

    count = nz - 1
    for way in flat_ways:
        count = count + has(way).astype(jnp.int32)

    lane = lax.broadcasted_iota(jnp.int32, (total, lanes), 1)

    def in_group(lane, group):
        return jnp.bitwise_and(lane + (3 + lanes) - 8 * group, lanes - 1) < 6

    own.wait()

    def pack(z, kept):
        mask = in_group(lane[:rows], z)
        return tuple(
            jnp.where(mask, pltpu.roll(box[v, 3 + z, EDGE:EDGE + rows, :], 8 * z, 1), kept[v])
            for v in range(2))

    empty = jnp.zeros((rows, lanes), jnp.float32)
    packed = lax.fori_loop(0, depth, pack, (empty, empty))
    for v in range(2):
        own_strips[v, EDGE:EDGE + rows, :] = packed[v]

    pl.semaphore_wait(barrier, count)
    strip_ways = [way for way in flat_ways if way[1]]
    for step in sides:
        begin("planes", lies(2, step))
    for way in strip_ways:
        begin("strips", way)
    for step in sides:
        begin("rows", lies(0, step))

    def merged(left, right):
        here = jnp.bitwise_and(lax.broadcasted_iota(jnp.int32, left.shape, 1), 7)
        return jnp.where(here >= 4, left, right)

    def along_y(v, plane, at, count, group, strips):
        here = lane[:count]
        block = box[v, plane, at:at + count, :]
        halo = pltpu.roll(strips, lanes - 8 * group, 1)

        def place(o):
            if o == 0:
                return block
            if o > 0:
                return pltpu.roll(jnp.where(here < o, halo, block), lanes - o, 1)
            return pltpu.roll(jnp.where(here >= lanes + o, halo, block), -o, 1)

        return both_of(place) if v == 0 else (smooth_of(place),)

    def own_y(blocks, planes):
        def turn(i, carry):
            done = []
            for p in range(planes):
                z = i * planes + p
                for at, count in blocks:
                    found = []
                    for v in range(2):
                        found += along_y(v, z + 3, at, count, z, joined[v, at:at + count, :])
                    done.append((z + 3, at, count, found))
            for plane, at, count, found in done:
                for k in range(3):
                    rows_done[k, plane, at:at + count, :] = found[k]
            return carry
        lax.fori_loop(0, depth // planes, turn, 0)

    def along_x(plane):
        width = 32 if rows % 32 == 0 else EDGE
        for at in range(0, rows, width):
            def reader(k):
                return lambda o: rows_done[k, plane, EDGE + at + o:EDGE + at + o + width, :]
            plain, steep = both_of(reader(0))
            crossed, other = smooth_of(reader(1)), smooth_of(reader(2))
            for k, found in enumerate((plain, steep, crossed, other)):
                flat_done[k, plane, at:at + width, :] = found

    def own_x(z, carry):
        along_x(z + 3)
        return carry

    for step, name in ((-1, "low"), (1, "high")):
        got("rows", lies(0, step))
        for side in sides:
            begin(name, lies(2, side))
    for way in strip_ways:
        got("strips", way)
    for v in range(2):
        joined[v] = merged(got_own[0, v], got_own[1, v])
    for step in sides:
        plane = 0 if step < 0 else depth - 3
        second = jnp.logical_and(lane >= 40, lane < 104)
        rim_strips[0 if step < 0 else 1] = jnp.where(
            second, pltpu.roll(joined[1], (8 * (8 - plane)) % lanes, 1),
            pltpu.roll(joined[0], (8 * (lanes // 8 - plane)) % lanes, 1))
        begin("rims", lies(2, step))
    own_y([(at, 40) for at in range(0, total, 40)], 1)
    lax.fori_loop(0, depth, own_x, 0)

    rims = {-1: ((0, 0), (1, 1), (2, 2)), 1: tuple((h, depth + 3 + h) for h in range(3))}

    def sample(z, at, chunk):
        def reader(k):
            return lambda o: flat_done[k, z + 3 + o, pl.ds(at, chunk), :]
        value, grad_z = both_of(reader(0))
        grad_x = smooth_of(reader(1))
        grad_y = smooth_of(reader(2))
        mixture = smooth_of(reader(3))
        position = 0.5 * (lanes - 1) + (0.5 * (lanes - 1)) * jnp.tanh(0.5 * value)
        index = jnp.minimum(position.astype(jnp.int32), lanes - 2)
        share = position - index.astype(jnp.float32)

        def look(c):
            low = jnp.take_along_axis(table[2 * c, :chunk], index, axis=1, mode="promise_in_bounds")
            rise = jnp.take_along_axis(table[2 * c + 1, :chunk], index, axis=1, mode="promise_in_bounds")
            return low + share * rise

        facing = grad_x * light[0, :chunk] + grad_y * light[1, :chunk] + grad_z * light[2, :chunk]
        square = grad_x * grad_x + grad_y * grad_y + grad_z * grad_z + SHADE_FLOOR
        shade = 0.25 + 0.75 * (facing * facing / square)
        alpha = 1.0 - jnp.exp((-0.5 * OPTICAL * depth_step) * look(3) * (1.0 + jnp.tanh(0.5 * mixture)))
        lit = alpha * shade
        return (lit * look(0), lit * look(1), lit * look(2), alpha)

    def over(front, back):
        left = 1.0 - front[3]
        return tuple(f + left * b for f, b in zip(front, back))

    def nothing(chunk):
        return tuple(jnp.zeros((chunk, lanes), jnp.float32) for _ in range(4))

    wide = light.shape[1]

    height = rows // nz
    inner_rows = min(height, wide)

    def inner_slab(slab):
        def inner_chunk(c, carry):
            at = pl.multiple_of(slab * height + c * inner_rows, inner_rows)

            def turn(i, acc):
                z = 3 + 2 * i
                pair = [sample(z + p, at, inner_rows) for p in range(2)]
                return over(acc, over(*pair))

            result = lax.fori_loop(0, (depth - 6) // 2, turn, nothing(inner_rows))
            for k in range(4):
                inner[k, pl.ds(at, inner_rows), :] = result[k]
            return carry

        lax.fori_loop(0, height // inner_rows, inner_chunk, 0)

    for j in range(1, nz):
        inner_slab(lax.rem(iz + j, nz))

    for step in sides:
        for name in ("planes", "low", "high", "rims"):
            got(name, lies(2, step))

    for step in sides:
        @pl.when(has(lies(2, step)))
        def _():
            for h, plane in rims[step]:
                for at in range(0, total, 40):
                    found = []
                    for v in range(2):
                        found += along_y(v, plane, at, 40, 8 * v + h, got_rim[0 if step < 0 else 1, at:at + 40, :])
                    for k in range(3):
                        rows_done[k, plane, at:at + 40, :] = found[k]
            for h, plane in rims[step]:
                along_x(plane)

    def slab_copy(j):
        return pltpu.make_async_remote_copy(
            src_ref=stage.at[j - 1], dst_ref=slabs.at[iz], send_sem=slab_send.at[j - 1],
            recv_sem=slab_recv.at[iz], device_id={"gz": lax.rem(iz + j, nz)}, device_id_type=MESH)

    for j in range(1, nz + 1):
        slab = lax.rem(iz + j, nz)
        if j == nz:
            inner_slab(slab)

        at = pl.multiple_of(slab * height, height)
        acc = sample(0, at, height)
        for z in (1, 2):
            acc = over(acc, sample(z, at, height))
        acc = over(acc, tuple(inner[k, pl.ds(at, height), :] for k in range(4)))
        for z in range(depth - 3, depth):
            acc = over(acc, sample(z, at, height))
        for k in range(4):
            if j < nz:
                stage[j - 1, k] = acc[k]
            else:
                slabs[iz, k] = acc[k]
        if j < nz:
            slab_copy(j).start()

    for j in range(1, nz):
        source = lax.rem(iz + j, nz)
        pltpu.make_async_remote_copy(
            src_ref=stage.at[j - 1], dst_ref=slabs.at[source], send_sem=slab_send.at[j - 1],
            recv_sem=slab_recv.at[source], device_id={"gz": source}, device_id_type=MESH).wait_recv()

    image = tuple(slabs[0, k] for k in range(4))
    for k in range(1, nz):
        image = over(image, tuple(slabs[k, c] for c in range(4)))
    for c in range(4):
        out[c] = image[c]

    for name, way in links:
        sent(name, way)
    for j in range(1, nz):
        slab_copy(j).wait_send()


def shards(sizes, field, transfer, light_angles):
    nx, ny, nz = sizes
    _, depth, rows, lanes = field.shape
    total = rows + 2 * EDGE
    height = rows // nz
    chunk = 32
    full = depth + 6
    f32 = jnp.float32
    return pl.pallas_call(
        functools.partial(kernel, sizes, 1.0 / (depth * nz)),
        out_shape=jax.ShapeDtypeStruct((4, height, lanes), f32),
        in_specs=[
            pl.BlockSpec(memory_space=pltpu.HBM),
            pl.BlockSpec(memory_space=pltpu.HBM),
            pl.BlockSpec(memory_space=pltpu.HBM),
        ],
        out_specs=pl.BlockSpec(memory_space=pltpu.VMEM),
        scratch_shapes=[
            pltpu.VMEM((4, lanes), f32),
            pltpu.SMEM((2,), f32),
            pltpu.VMEM((2, full, total, lanes), f32),
            pltpu.VMEM((2, total, lanes), f32),
            pltpu.VMEM((2, total, lanes), f32),
            pltpu.VMEM((2, 2, total, lanes), f32),
            pltpu.VMEM((2, total, lanes), f32),
            pltpu.VMEM((2, total, lanes), f32),
            pltpu.VMEM((3, full, total, lanes), f32),
            pltpu.VMEM((4, full, rows, lanes), f32),
            pltpu.VMEM((8, chunk, lanes), f32),
            pltpu.VMEM((3, chunk, lanes), f32),
            pltpu.VMEM((4, rows, lanes), f32),
            pltpu.VMEM((nz - 1, 4, height, lanes), f32),
            pltpu.VMEM((nz, 4, height, lanes), f32),
            pltpu.SemaphoreType.DMA,
            pltpu.SemaphoreType.DMA((2,)),
            pltpu.SemaphoreType.DMA((20,)),
            pltpu.SemaphoreType.DMA((20,)),
            pltpu.SemaphoreType.DMA((nz,)),
            pltpu.SemaphoreType.DMA((nz,)),
        ],
        compiler_params=pltpu.CompilerParams(
            collective_id=0, has_side_effects=True, vmem_limit_bytes=40 * 1024 * 1024),
    )(*(pltpu.with_memory_space_constraint(x, pltpu.HBM) for x in (field, transfer, light_angles)))


def solution(mesh):
    sizes = tuple(mesh.shape[name] for name in ("gx", "gy", "gz"))
    placed = (P(None, "gz", "gx", "gy"), P(), P())
    return jax.shard_map(
        functools.partial(shards, sizes), mesh=mesh, in_specs=placed,
        out_specs=P(None, ("gx", "gz"), "gy"), check_vma=False
    )
```

```python
import functools
import math

import jax
import jax.numpy as jnp
from jax import lax
from jax.experimental import pallas as pl
from jax.experimental.pallas import tpu as pltpu
from jax.sharding import PartitionSpec as P

MESH = pl.DeviceIdType.MESH
SIGMA_TAPS = 1.2
OPTICAL = 2.0
SHADE_FLOOR = 0.25
EDGE = 8


def filter_taps():
    places = [-3, -2, -1, 0, 1, 2, 3]
    bell = [math.exp(-place * place / (2.0 * SIGMA_TAPS * SIGMA_TAPS)) for place in places]
    bell_total = sum(bell)
    slope_total = sum((place * place * weight for place, weight in zip(places, bell)))
    smooth_taps = [weight / bell_total for weight in bell]
    slope_taps = [place * weight / slope_total for place, weight in zip(places, bell)]
    return (smooth_taps, slope_taps)


def smooth_of(at):
    taps, _ = filter_taps()
    total = taps[3] * at(0)
    for o in (1, 2, 3):
        total = total + taps[3 + o] * (at(o) + at(-o))
    return total


def slope_of(at):
    _, taps = filter_taps()
    total = taps[4] * (at(1) - at(-1))
    for o in (2, 3):
        total = total + taps[3 + o] * (at(o) - at(-o))
    return total


def both_of(at):
    smooth, slope = filter_taps()
    plain, steep = smooth[3] * at(0), None
    for o in (1, 2, 3):
        after, before = at(o), at(-o)
        plain = plain + smooth[3 + o] * (after + before)
        term = slope[3 + o] * (after - before)
        steep = term if steep is None else steep + term
    return plain, steep


def kernel(sizes, depth_step, field, transfer_in, angles_in, out, transfer, angles, box, own_strips, rim_strips, got_own, got_rim, joined,
           rows_done, flat_done, table, light, inner, stage, slabs,
           local_sem, small_sem, send_sem, recv_sem, slab_send, slab_recv):
    nx, ny, nz = sizes
    _, depth, rows, lanes = field.shape
    total = rows + 2 * EDGE
    ix, iy, iz = (lax.axis_index(name) for name in ("gx", "gy", "gz"))
    spots = (("gx", ix, nx), ("gy", iy, ny), ("gz", iz, nz))

    def has(way):
        need = None
        for (_, place, count), step in zip(spots, way):
            if step:
                here = place > 0 if step < 0 else place < count - 1
                need = here if need is None else jnp.logical_and(need, here)
        return need

    def target(way):
        return {name: place + step for (name, place, _), step in zip(spots, way) if step}

    def lies(axis, step):
        return tuple(step if k == axis else 0 for k in range(3))

    flat_ways = [(dx, dy, 0) for dx in (-1, 0, 1) for dy in (-1, 0, 1) if dx or dy]
    sides = (-1, 1)

    barrier = pltpu.get_barrier_semaphore()
    for way in flat_ways:
        @pl.when(has(way))
        def _():
            pl.semaphore_signal(barrier, inc=1, device_id=target(way), device_id_type=MESH)
    for j in range(1, nz):
        pl.semaphore_signal(barrier, inc=1, device_id={"gz": lax.rem(iz + j, nz)}, device_id_type=MESH)

    own = pltpu.make_async_copy(
        field, box.at[:, pl.ds(3, depth), pl.ds(EDGE, rows), :], local_sem)
    own.start()
    small = (pltpu.make_async_copy(transfer_in, transfer, small_sem.at[0]),
             pltpu.make_async_copy(angles_in, angles, small_sem.at[1]))
    for each in small:
        each.start()

    for step in sides:
        edge = 0 if step < 0 else EDGE + rows
        @pl.when(jnp.logical_not(has(lies(0, step))))
        def _():
            box[:, :, edge:edge + EDGE, :] = jnp.zeros((2, depth + 6, EDGE, lanes), jnp.float32)
            got_own[:, :, edge:edge + EDGE, :] = jnp.zeros((2, 2, EDGE, lanes), jnp.float32)
        first = 0 if step < 0 else depth + 3
        @pl.when(jnp.logical_not(has(lies(2, step))))
        def _():
            flat_done[:, first:first + 3] = jnp.zeros((4, 3, rows, lanes), jnp.float32)
        side = 0 if step < 0 else 1
        @pl.when(jnp.logical_not(has(lies(1, step))))
        def _():
            got_own[side] = jnp.zeros((2, total, lanes), jnp.float32)

    links = {}

    def link(name, way, src, dst, need=None):
        links[name, way] = (len(links), src, dst, need)

    def wanted(name, way):
        need, more = has(way), links[name, way][3]
        return need if more is None else jnp.logical_and(need, more)

    def copy(name, way):
        slot, src, dst, _ = links[name, way]
        return pltpu.make_async_remote_copy(
            src_ref=src, dst_ref=dst, send_sem=send_sem.at[slot], recv_sem=recv_sem.at[slot],
            device_id=target(way), device_id_type=MESH)

    def begin(name, way):
        @pl.when(wanted(name, way))
        def _():
            copy(name, way).start()

    def sent(name, way):
        @pl.when(wanted(name, way))
        def _():
            copy(name, way).wait_send()

    def got(name, way):
        back = tuple(-step for step in way)
        need, more = has(way), links[name, back][3]
        @pl.when(need if more is None else jnp.logical_and(need, more))
        def _():
            copy(name, back).wait_recv()

    every = pl.ds(3, depth)
    middle = pl.ds(EDGE, rows)

    def rows_from(dx):
        return middle if dx == 0 else pl.ds(EDGE if dx < 0 else rows, EDGE)

    def rows_to(dx):
        return middle if dx == 0 else pl.ds(EDGE + rows if dx < 0 else 0, EDGE)

    for way in flat_ways:
        if way[1]:
            side = 0 if way[1] > 0 else 1
            link("strips", way, own_strips.at[:, rows_from(way[0]), :], got_own.at[side, :, rows_to(way[0]), :])
    for step in sides:
        row = 0 if step < 0 else rows - EDGE
        link("rows", lies(0, step), field.at[:, :, pl.ds(row, EDGE), :], box.at[:, every, rows_to(step), :])
        plane = 0 if step < 0 else depth - 3
        to = depth + 3 if step < 0 else 0
        link("planes", lies(2, step), field.at[:, pl.ds(plane, 3)], box.at[:, pl.ds(to, 3), middle, :])
        for name, at, side in (("low", 0, -1), ("high", EDGE + rows, 1)):
            link(name, lies(2, step), box.at[:, pl.ds(3 + plane, 3), pl.ds(at, EDGE), :],
                 box.at[:, pl.ds(to, 3), pl.ds(at, EDGE), :], has(lies(0, side)))
        link("rims", lies(2, step), rim_strips.at[0 if step < 0 else 1], got_rim.at[0 if step > 0 else 1])

    count = nz - 1
    for way in flat_ways:
        count = count + has(way).astype(jnp.int32)

    lane = lax.broadcasted_iota(jnp.int32, (total, lanes), 1)

    def in_group(lane, group):
        return jnp.bitwise_and(lane + (3 + lanes) - 8 * group, lanes - 1) < 6

    pl.semaphore_wait(barrier, count)
    for step in sides:
        begin("planes", lies(2, step))
    for step in sides:
        begin("rows", lies(0, step))
    own.wait()
    group_count = 4 if depth % 4 == 0 else 1

    def pack(i, kept):
        for p in range(group_count):
            z = i * group_count + p
            mask = in_group(lane[:rows], z)
            kept = tuple(
                jnp.where(mask, pltpu.roll(box[v, 3 + z, EDGE:EDGE + rows, :], 8 * z, 1), kept[v])
                for v in range(2))
        return kept

    empty = jnp.zeros((rows, lanes), jnp.float32)
    packed = lax.fori_loop(0, depth // group_count, pack, (empty, empty))
    for v in range(2):
        own_strips[v, EDGE:EDGE + rows, :] = packed[v]

    strip_ways = [way for way in flat_ways if way[1]]
    for way in strip_ways:
        begin("strips", way)

    for each in small:
        each.wait()
    azimuth = jnp.full(light.shape[1:], angles[0], jnp.float32)
    polar = jnp.full(light.shape[1:], angles[1], jnp.float32)
    light[0] = jnp.cos(azimuth) * jnp.sin(polar)
    light[1] = jnp.sin(azimuth) * jnp.sin(polar)
    light[2] = jnp.cos(polar)
    for c in range(4):
        line = jnp.broadcast_to(transfer[c:c + 1, :], table.shape[1:])
        table[2 * c] = line
        table[2 * c + 1] = pltpu.roll(line, lanes - 1, 1) - line

    def merged(left, right):
        here = jnp.bitwise_and(lax.broadcasted_iota(jnp.int32, left.shape, 1), 7)
        return jnp.where(here >= 4, left, right)

    def along_y(v, plane, at, count, group, strips):
        here = lane[:count]
        block = box[v, plane, at:at + count, :]
        halo = pltpu.roll(strips, lanes - 8 * group, 1)

        def place(o):
            if o == 0:
                return block
            if o > 0:
                return pltpu.roll(jnp.where(here < o, halo, block), lanes - o, 1)
            return pltpu.roll(jnp.where(here >= lanes + o, halo, block), -o, 1)

        return both_of(place) if v == 0 else (smooth_of(place),)

    def own_y(blocks, planes):
        def turn(i, carry):
            done = []
            for p in range(planes):
                z = i * planes + p
                for at, count in blocks:
                    found = []
                    for v in range(2):
                        found += along_y(v, z + 3, at, count, z, joined[v, at:at + count, :])
                    done.append((z + 3, at, count, found))
            for plane, at, count, found in done:
                for k in range(3):
                    rows_done[k, plane, at:at + count, :] = found[k]
            return carry
        lax.fori_loop(0, depth // planes, turn, 0)

    def along_x(plane):
        width = 32 if rows % 32 == 0 else EDGE
        for at in range(0, rows, width):
            def reader(k):
                return lambda o: rows_done[k, plane, EDGE + at + o:EDGE + at + o + width, :]
            plain, steep = both_of(reader(0))
            crossed, other = smooth_of(reader(1)), smooth_of(reader(2))
            for k, found in enumerate((plain, steep, crossed, other)):
                flat_done[k, plane, at:at + width, :] = found

    def own_x(z, carry):
        along_x(z + 3)
        return carry

    for step, name in ((-1, "low"), (1, "high")):
        got("rows", lies(0, step))
        for side in sides:
            begin(name, lies(2, side))
    for way in strip_ways:
        got("strips", way)
    for v in range(2):
        joined[v] = merged(got_own[0, v], got_own[1, v])
    for step in sides:
        plane = 0 if step < 0 else depth - 3
        second = jnp.logical_and(lane >= 40, lane < 104)
        rim_strips[0 if step < 0 else 1] = jnp.where(
            second, pltpu.roll(joined[1], (8 * (8 - plane)) % lanes, 1),
            pltpu.roll(joined[0], (8 * (lanes // 8 - plane)) % lanes, 1))
        begin("rims", lies(2, step))
    own_y([(at, 40) for at in range(0, total, 40)], 1)
    lax.fori_loop(0, depth, own_x, 0)

    rims = {-1: ((0, 0), (1, 1), (2, 2)), 1: tuple((h, depth + 3 + h) for h in range(3))}

    def sample(z, at, chunk):
        def reader(k):
            return lambda o: flat_done[k, z + 3 + o, pl.ds(at, chunk), :]
        value, grad_z = both_of(reader(0))
        grad_x = smooth_of(reader(1))
        grad_y = smooth_of(reader(2))
        mixture = smooth_of(reader(3))
        position = 0.5 * (lanes - 1) + (0.5 * (lanes - 1)) * jnp.tanh(0.5 * value)
        index = jnp.minimum(position.astype(jnp.int32), lanes - 2)
        share = position - index.astype(jnp.float32)

        def look(c):
            low = jnp.take_along_axis(table[2 * c, :chunk], index, axis=1, mode="promise_in_bounds")
            rise = jnp.take_along_axis(table[2 * c + 1, :chunk], index, axis=1, mode="promise_in_bounds")
            return low + share * rise

        facing = grad_x * light[0, :chunk] + grad_y * light[1, :chunk] + grad_z * light[2, :chunk]
        square = grad_x * grad_x + grad_y * grad_y + grad_z * grad_z + SHADE_FLOOR
        shade = 0.25 + 0.75 * (facing * facing / square)
        alpha = 1.0 - jnp.exp((-0.5 * OPTICAL * depth_step) * look(3) * (1.0 + jnp.tanh(0.5 * mixture)))
        lit = alpha * shade
        return (lit * look(0), lit * look(1), lit * look(2), alpha)

    def over(front, back):
        left = 1.0 - front[3]
        return tuple(f + left * b for f, b in zip(front, back))

    def nothing(chunk):
        return tuple(jnp.zeros((chunk, lanes), jnp.float32) for _ in range(4))

    wide = light.shape[1]

    height = rows // nz
    inner_rows = min(height, wide)

    def inner_slab(slab):
        def inner_chunk(c, carry):
            at = pl.multiple_of(slab * height + c * inner_rows, inner_rows)

            def turn(i, acc):
                z = 3 + 2 * i
                pair = [sample(z + p, at, inner_rows) for p in range(2)]
                return over(acc, over(*pair))

            result = lax.fori_loop(0, (depth - 6) // 2, turn, nothing(inner_rows))
            for k in range(4):
                inner[k, pl.ds(at, inner_rows), :] = result[k]
            return carry

        lax.fori_loop(0, height // inner_rows, inner_chunk, 0)

    for j in range(1, nz):
        inner_slab(lax.rem(iz + j, nz))

    for step in sides:
        for name in ("planes", "low", "high", "rims"):
            got(name, lies(2, step))

    for step in sides:
        @pl.when(has(lies(2, step)))
        def _():
            for h, plane in rims[step]:
                for at in range(0, total, 40):
                    found = []
                    for v in range(2):
                        found += along_y(v, plane, at, 40, 8 * v + h, got_rim[0 if step < 0 else 1, at:at + 40, :])
                    for k in range(3):
                        rows_done[k, plane, at:at + 40, :] = found[k]
            for h, plane in rims[step]:
                along_x(plane)

    def slab_copy(j):
        return pltpu.make_async_remote_copy(
            src_ref=stage.at[j - 1], dst_ref=slabs.at[iz], send_sem=slab_send.at[j - 1],
            recv_sem=slab_recv.at[iz], device_id={"gz": lax.rem(iz + j, nz)}, device_id_type=MESH)

    for j in range(1, nz + 1):
        slab = lax.rem(iz + j, nz)
        if j == nz:
            inner_slab(slab)

        at = pl.multiple_of(slab * height, height)
        acc = sample(0, at, height)
        for z in (1, 2):
            acc = over(acc, sample(z, at, height))
        acc = over(acc, tuple(inner[k, pl.ds(at, height), :] for k in range(4)))
        for z in range(depth - 3, depth):
            acc = over(acc, sample(z, at, height))
        for k in range(4):
            if j < nz:
                stage[j - 1, k] = acc[k]
            else:
                slabs[iz, k] = acc[k]
        if j < nz:
            slab_copy(j).start()

    for j in range(1, nz):
        source = lax.rem(iz + j, nz)
        pltpu.make_async_remote_copy(
            src_ref=stage.at[j - 1], dst_ref=slabs.at[source], send_sem=slab_send.at[j - 1],
            recv_sem=slab_recv.at[source], device_id={"gz": source}, device_id_type=MESH).wait_recv()

    image = tuple(slabs[0, k] for k in range(4))
    for k in range(1, nz):
        image = over(image, tuple(slabs[k, c] for c in range(4)))
    for c in range(4):
        out[c] = image[c]

    for name, way in links:
        sent(name, way)
    for j in range(1, nz):
        slab_copy(j).wait_send()


def shards(sizes, field, transfer, light_angles):
    nx, ny, nz = sizes
    _, depth, rows, lanes = field.shape
    total = rows + 2 * EDGE
    height = rows // nz
    chunk = 32
    full = depth + 6
    f32 = jnp.float32
    return pl.pallas_call(
        functools.partial(kernel, sizes, 1.0 / (depth * nz)),
        out_shape=jax.ShapeDtypeStruct((4, height, lanes), f32),
        in_specs=[
            pl.BlockSpec(memory_space=pltpu.HBM),
            pl.BlockSpec(memory_space=pltpu.HBM),
            pl.BlockSpec(memory_space=pltpu.HBM),
        ],
        out_specs=pl.BlockSpec(memory_space=pltpu.VMEM),
        scratch_shapes=[
            pltpu.VMEM((4, lanes), f32),
            pltpu.SMEM((2,), f32),
            pltpu.VMEM((2, full, total, lanes), f32),
            pltpu.VMEM((2, total, lanes), f32),
            pltpu.VMEM((2, total, lanes), f32),
            pltpu.VMEM((2, 2, total, lanes), f32),
            pltpu.VMEM((2, total, lanes), f32),
            pltpu.VMEM((2, total, lanes), f32),
            pltpu.VMEM((3, full, total, lanes), f32),
            pltpu.VMEM((4, full, rows, lanes), f32),
            pltpu.VMEM((8, chunk, lanes), f32),
            pltpu.VMEM((3, chunk, lanes), f32),
            pltpu.VMEM((4, rows, lanes), f32),
            pltpu.VMEM((nz - 1, 4, height, lanes), f32),
            pltpu.VMEM((nz, 4, height, lanes), f32),
            pltpu.SemaphoreType.DMA,
            pltpu.SemaphoreType.DMA((2,)),
            pltpu.SemaphoreType.DMA((20,)),
            pltpu.SemaphoreType.DMA((20,)),
            pltpu.SemaphoreType.DMA((nz,)),
            pltpu.SemaphoreType.DMA((nz,)),
        ],
        compiler_params=pltpu.CompilerParams(
            collective_id=0, has_side_effects=True, vmem_limit_bytes=40 * 1024 * 1024),
    )(*(pltpu.with_memory_space_constraint(x, pltpu.HBM) for x in (field, transfer, light_angles)))


def solution(mesh):
    sizes = tuple(mesh.shape[name] for name in ("gx", "gy", "gz"))
    placed = (P(None, "gz", "gx", "gy"), P(), P())
    return jax.shard_map(
        functools.partial(shards, sizes), mesh=mesh, in_specs=placed,
        out_specs=P(None, ("gx", "gz"), "gy"), check_vma=False
    )
```

```python
import functools
import math

import jax
import jax.numpy as jnp
from jax import lax
from jax.experimental import pallas as pl
from jax.experimental.pallas import tpu as pltpu
from jax.sharding import PartitionSpec as P

MESH = pl.DeviceIdType.MESH
SIGMA_TAPS = 1.2
OPTICAL = 2.0
SHADE_FLOOR = 0.25
EDGE = 8


def filter_taps():
    places = [-3, -2, -1, 0, 1, 2, 3]
    bell = [math.exp(-place * place / (2.0 * SIGMA_TAPS * SIGMA_TAPS)) for place in places]
    bell_total = sum(bell)
    slope_total = sum((place * place * weight for place, weight in zip(places, bell)))
    smooth_taps = [weight / bell_total for weight in bell]
    slope_taps = [place * weight / slope_total for place, weight in zip(places, bell)]
    return (smooth_taps, slope_taps)


def smooth_of(at):
    taps, _ = filter_taps()
    total = taps[3] * at(0)
    for o in (1, 2, 3):
        total = total + taps[3 + o] * (at(o) + at(-o))
    return total


def slope_of(at):
    _, taps = filter_taps()
    total = taps[4] * (at(1) - at(-1))
    for o in (2, 3):
        total = total + taps[3 + o] * (at(o) - at(-o))
    return total


def both_of(at):
    smooth, slope = filter_taps()
    plain, steep = smooth[3] * at(0), None
    for o in (1, 2, 3):
        after, before = at(o), at(-o)
        plain = plain + smooth[3 + o] * (after + before)
        term = slope[3 + o] * (after - before)
        steep = term if steep is None else steep + term
    return plain, steep


def kernel(sizes, depth_step, field, transfer_in, angles_in, out, transfer, angles, box, own_strips, rim_strips, got_own, got_rim, joined,
           rows_done, flat_done, table, light, inner, stage, slabs,
           local_sem, small_sem, send_sem, recv_sem, slab_send, slab_recv):
    nx, ny, nz = sizes
    _, depth, rows, lanes = field.shape
    total = rows + 2 * EDGE
    ix, iy, iz = (lax.axis_index(name) for name in ("gx", "gy", "gz"))
    spots = (("gx", ix, nx), ("gy", iy, ny), ("gz", iz, nz))

    def has(way):
        need = None
        for (_, place, count), step in zip(spots, way):
            if step:
                here = place > 0 if step < 0 else place < count - 1
                need = here if need is None else jnp.logical_and(need, here)
        return need

    def target(way):
        return {name: place + step for (name, place, _), step in zip(spots, way) if step}

    def lies(axis, step):
        return tuple(step if k == axis else 0 for k in range(3))

    flat_ways = [(dx, dy, 0) for dx in (-1, 0, 1) for dy in (-1, 0, 1) if dx or dy]
    sides = (-1, 1)

    barrier = pltpu.get_barrier_semaphore()
    for way in flat_ways:
        @pl.when(has(way))
        def _():
            pl.semaphore_signal(barrier, inc=1, device_id=target(way), device_id_type=MESH)
    for j in range(1, nz):
        pl.semaphore_signal(barrier, inc=1, device_id={"gz": lax.rem(iz + j, nz)}, device_id_type=MESH)

    own = pltpu.make_async_copy(
        field, box.at[:, pl.ds(3, depth), pl.ds(EDGE, rows), :], local_sem)
    own.start()
    small = (pltpu.make_async_copy(transfer_in, transfer, small_sem.at[0]),
             pltpu.make_async_copy(angles_in, angles, small_sem.at[1]))
    for each in small:
        each.start()

    for step in sides:
        edge = 0 if step < 0 else EDGE + rows
        @pl.when(jnp.logical_not(has(lies(0, step))))
        def _():
            box[:, :, edge:edge + EDGE, :] = jnp.zeros((2, depth + 6, EDGE, lanes), jnp.float32)
            got_own[:, :, edge:edge + EDGE, :] = jnp.zeros((2, 2, EDGE, lanes), jnp.float32)
        first = 0 if step < 0 else depth + 3
        @pl.when(jnp.logical_not(has(lies(2, step))))
        def _():
            flat_done[:, first:first + 3] = jnp.zeros((4, 3, rows, lanes), jnp.float32)
        side = 0 if step < 0 else 1
        @pl.when(jnp.logical_not(has(lies(1, step))))
        def _():
            got_own[side] = jnp.zeros((2, total, lanes), jnp.float32)

    links = {}

    def link(name, way, src, dst, need=None):
        links[name, way] = (len(links), src, dst, need)

    def wanted(name, way):
        need, more = has(way), links[name, way][3]
        return need if more is None else jnp.logical_and(need, more)

    def copy(name, way):
        slot, src, dst, _ = links[name, way]
        return pltpu.make_async_remote_copy(
            src_ref=src, dst_ref=dst, send_sem=send_sem.at[slot], recv_sem=recv_sem.at[slot],
            device_id=target(way), device_id_type=MESH)

    def begin(name, way):
        @pl.when(wanted(name, way))
        def _():
            copy(name, way).start()

    def sent(name, way):
        @pl.when(wanted(name, way))
        def _():
            copy(name, way).wait_send()

    def got(name, way):
        back = tuple(-step for step in way)
        need, more = has(way), links[name, back][3]
        @pl.when(need if more is None else jnp.logical_and(need, more))
        def _():
            copy(name, back).wait_recv()

    every = pl.ds(3, depth)
    middle = pl.ds(EDGE, rows)

    def rows_from(dx):
        return middle if dx == 0 else pl.ds(EDGE if dx < 0 else rows, EDGE)

    def rows_to(dx):
        return middle if dx == 0 else pl.ds(EDGE + rows if dx < 0 else 0, EDGE)

    for way in flat_ways:
        if way[1]:
            side = 0 if way[1] > 0 else 1
            link("strips", way, own_strips.at[:, rows_from(way[0]), :], got_own.at[side, :, rows_to(way[0]), :])
    for step in sides:
        row = 0 if step < 0 else rows - EDGE
        link("rows", lies(0, step), field.at[:, :, pl.ds(row, EDGE), :], box.at[:, every, rows_to(step), :])
        plane = 0 if step < 0 else depth - 3
        to = depth + 3 if step < 0 else 0
        link("planes", lies(2, step), field.at[:, pl.ds(plane, 3)], box.at[:, pl.ds(to, 3), middle, :])
        for name, at, side in (("low", 0, -1), ("high", EDGE + rows, 1)):
            link(name, lies(2, step), box.at[:, pl.ds(3 + plane, 3), pl.ds(at, EDGE), :],
                 box.at[:, pl.ds(to, 3), pl.ds(at, EDGE), :], has(lies(0, side)))
        link("rims", lies(2, step), rim_strips.at[0 if step < 0 else 1], got_rim.at[0 if step > 0 else 1])

    count = nz - 1
    for way in flat_ways:
        count = count + has(way).astype(jnp.int32)

    lane = lax.broadcasted_iota(jnp.int32, (total, lanes), 1)

    def in_group(lane, group):
        return jnp.bitwise_and(lane + (3 + lanes) - 8 * group, lanes - 1) < 6

    pl.semaphore_wait(barrier, count)
    for step in sides:
        begin("planes", lies(2, step))
    for step in sides:
        begin("rows", lies(0, step))
    own.wait()
    group_count = 4 if depth % 4 == 0 else 1

    def pack(i, kept):
        for p in range(group_count):
            z = i * group_count + p
            mask = in_group(lane[:rows], z)
            kept = tuple(
                jnp.where(mask, pltpu.roll(box[v, 3 + z, EDGE:EDGE + rows, :], 8 * z, 1), kept[v])
                for v in range(2))
        return kept

    empty = jnp.zeros((rows, lanes), jnp.float32)
    packed = lax.fori_loop(0, depth // group_count, pack, (empty, empty))
    for v in range(2):
        own_strips[v, EDGE:EDGE + rows, :] = packed[v]

    strip_ways = [way for way in flat_ways if way[1]]
    for way in strip_ways:
        begin("strips", way)

    for each in small:
        each.wait()
    azimuth = jnp.full(light.shape[1:], angles[0], jnp.float32)
    polar = jnp.full(light.shape[1:], angles[1], jnp.float32)
    light[0] = jnp.cos(azimuth) * jnp.sin(polar)
    light[1] = jnp.sin(azimuth) * jnp.sin(polar)
    light[2] = jnp.cos(polar)
    for c in range(4):
        line = jnp.broadcast_to(transfer[c:c + 1, :], table.shape[1:])
        table[2 * c] = line
        table[2 * c + 1] = pltpu.roll(line, lanes - 1, 1) - line

    def merged(left, right):
        here = jnp.bitwise_and(lax.broadcasted_iota(jnp.int32, left.shape, 1), 7)
        return jnp.where(here >= 4, left, right)

    def along_y(v, plane, at, count, group, strips):
        here = lane[:count]
        block = box[v, plane, at:at + count, :]
        halo = pltpu.roll(strips, lanes - 8 * group, 1)

        def place(o):
            if o == 0:
                return block
            if o > 0:
                return pltpu.roll(jnp.where(here < o, halo, block), lanes - o, 1)
            return pltpu.roll(jnp.where(here >= lanes + o, halo, block), -o, 1)

        return both_of(place) if v == 0 else (smooth_of(place),)

    def own_y(blocks, planes):
        def turn(i, carry):
            done = []
            for p in range(planes):
                z = i * planes + p
                for at, count in blocks:
                    found = []
                    for v in range(2):
                        found += along_y(v, z + 3, at, count, z, joined[v, at:at + count, :])
                    done.append((z + 3, at, count, found))
            for plane, at, count, found in done:
                for k in range(3):
                    rows_done[k, plane, at:at + count, :] = found[k]
            return carry
        lax.fori_loop(0, depth // planes, turn, 0)

    def along_x(plane):
        width = 32 if rows % 32 == 0 else EDGE
        for at in range(0, rows, width):
            def reader(k):
                return lambda o: rows_done[k, plane, EDGE + at + o:EDGE + at + o + width, :]
            plain, steep = both_of(reader(0))
            crossed, other = smooth_of(reader(1)), smooth_of(reader(2))
            for k, found in enumerate((plain, steep, crossed, other)):
                flat_done[k, plane, at:at + width, :] = found

    def own_x(z, carry):
        along_x(z + 3)
        return carry

    for step, name in ((-1, "low"), (1, "high")):
        got("rows", lies(0, step))
        for side in sides:
            begin(name, lies(2, side))
    for way in strip_ways:
        got("strips", way)
    for v in range(2):
        joined[v] = merged(got_own[0, v], got_own[1, v])
    for step in sides:
        plane = 0 if step < 0 else depth - 3
        second = jnp.logical_and(lane >= 40, lane < 104)
        rim_strips[0 if step < 0 else 1] = jnp.where(
            second, pltpu.roll(joined[1], (8 * (8 - plane)) % lanes, 1),
            pltpu.roll(joined[0], (8 * (lanes // 8 - plane)) % lanes, 1))
        begin("rims", lies(2, step))
    own_y([(at, 40) for at in range(0, total, 40)], 2 if depth % 2 == 0 else 1)
    lax.fori_loop(0, depth, own_x, 0)

    rims = {-1: ((0, 0), (1, 1), (2, 2)), 1: tuple((h, depth + 3 + h) for h in range(3))}

    def sample(z, at, chunk):
        def reader(k):
            return lambda o: flat_done[k, z + 3 + o, pl.ds(at, chunk), :]
        value, grad_z = both_of(reader(0))
        grad_x = smooth_of(reader(1))
        grad_y = smooth_of(reader(2))
        mixture = smooth_of(reader(3))
        position = 0.5 * (lanes - 1) + (0.5 * (lanes - 1)) * jnp.tanh(0.5 * value)
        index = jnp.minimum(position.astype(jnp.int32), lanes - 2)
        share = position - index.astype(jnp.float32)

        def look(c):
            low = jnp.take_along_axis(table[2 * c, :chunk], index, axis=1, mode="promise_in_bounds")
            rise = jnp.take_along_axis(table[2 * c + 1, :chunk], index, axis=1, mode="promise_in_bounds")
            return low + share * rise

        facing = grad_x * light[0, :chunk] + grad_y * light[1, :chunk] + grad_z * light[2, :chunk]
        square = grad_x * grad_x + grad_y * grad_y + grad_z * grad_z + SHADE_FLOOR
        shade = 0.25 + 0.75 * (facing * facing / square)
        alpha = 1.0 - jnp.exp((-0.5 * OPTICAL * depth_step) * look(3) * (1.0 + jnp.tanh(0.5 * mixture)))
        lit = alpha * shade
        return (lit * look(0), lit * look(1), lit * look(2), alpha)

    def over(front, back):
        left = 1.0 - front[3]
        return tuple(f + left * b for f, b in zip(front, back))

    def nothing(chunk):
        return tuple(jnp.zeros((chunk, lanes), jnp.float32) for _ in range(4))

    wide = light.shape[1]

    height = rows // nz
    inner_rows = min(height, wide)

    run = next(k for k in (5, 2, 1) if (depth - 6) % k == 0)

    def inner_slab(slab):
        def inner_chunk(c, carry):
            at = pl.multiple_of(slab * height + c * inner_rows, inner_rows)

            def turn(i, acc):
                for p in range(run):
                    acc = over(acc, sample(3 + run * i + p, at, inner_rows))
                return acc

            result = lax.fori_loop(0, (depth - 6) // run, turn, nothing(inner_rows))
            for k in range(4):
                inner[k, pl.ds(at, inner_rows), :] = result[k]
            return carry

        lax.fori_loop(0, height // inner_rows, inner_chunk, 0)

    for j in range(1, nz):
        inner_slab(lax.rem(iz + j, nz))

    for step in sides:
        for name in ("planes", "low", "high", "rims"):
            got(name, lies(2, step))

    for step in sides:
        @pl.when(has(lies(2, step)))
        def _():
            for h, plane in rims[step]:
                for at in range(0, total, 40):
                    found = []
                    for v in range(2):
                        found += along_y(v, plane, at, 40, 8 * v + h, got_rim[0 if step < 0 else 1, at:at + 40, :])
                    for k in range(3):
                        rows_done[k, plane, at:at + 40, :] = found[k]
            for h, plane in rims[step]:
                along_x(plane)

    def slab_copy(j):
        return pltpu.make_async_remote_copy(
            src_ref=stage.at[j - 1], dst_ref=slabs.at[iz], send_sem=slab_send.at[j - 1],
            recv_sem=slab_recv.at[iz], device_id={"gz": lax.rem(iz + j, nz)}, device_id_type=MESH)

    for j in range(1, nz + 1):
        slab = lax.rem(iz + j, nz)
        if j == nz:
            inner_slab(slab)

        at = pl.multiple_of(slab * height, height)
        acc = sample(0, at, height)
        for z in (1, 2):
            acc = over(acc, sample(z, at, height))
        acc = over(acc, tuple(inner[k, pl.ds(at, height), :] for k in range(4)))
        for z in range(depth - 3, depth):
            acc = over(acc, sample(z, at, height))
        for k in range(4):
            if j < nz:
                stage[j - 1, k] = acc[k]
            else:
                slabs[iz, k] = acc[k]
        if j < nz:
            slab_copy(j).start()

    for j in range(1, nz):
        source = lax.rem(iz + j, nz)
        pltpu.make_async_remote_copy(
            src_ref=stage.at[j - 1], dst_ref=slabs.at[source], send_sem=slab_send.at[j - 1],
            recv_sem=slab_recv.at[source], device_id={"gz": source}, device_id_type=MESH).wait_recv()

    image = tuple(slabs[0, k] for k in range(4))
    for k in range(1, nz):
        image = over(image, tuple(slabs[k, c] for c in range(4)))
    for c in range(4):
        out[c] = image[c]

    for name, way in links:
        sent(name, way)
    for j in range(1, nz):
        slab_copy(j).wait_send()


def shards(sizes, field, transfer, light_angles):
    nx, ny, nz = sizes
    _, depth, rows, lanes = field.shape
    total = rows + 2 * EDGE
    height = rows // nz
    chunk = 32
    full = depth + 6
    f32 = jnp.float32
    return pl.pallas_call(
        functools.partial(kernel, sizes, 1.0 / (depth * nz)),
        out_shape=jax.ShapeDtypeStruct((4, height, lanes), f32),
        in_specs=[
            pl.BlockSpec(memory_space=pltpu.HBM),
            pl.BlockSpec(memory_space=pltpu.HBM),
            pl.BlockSpec(memory_space=pltpu.HBM),
        ],
        out_specs=pl.BlockSpec(memory_space=pltpu.VMEM),
        scratch_shapes=[
            pltpu.VMEM((4, lanes), f32),
            pltpu.SMEM((2,), f32),
            pltpu.VMEM((2, full, total, lanes), f32),
            pltpu.VMEM((2, total, lanes), f32),
            pltpu.VMEM((2, total, lanes), f32),
            pltpu.VMEM((2, 2, total, lanes), f32),
            pltpu.VMEM((2, total, lanes), f32),
            pltpu.VMEM((2, total, lanes), f32),
            pltpu.VMEM((3, full, total, lanes), f32),
            pltpu.VMEM((4, full, rows, lanes), f32),
            pltpu.VMEM((8, chunk, lanes), f32),
            pltpu.VMEM((3, chunk, lanes), f32),
            pltpu.VMEM((4, rows, lanes), f32),
            pltpu.VMEM((nz - 1, 4, height, lanes), f32),
            pltpu.VMEM((nz, 4, height, lanes), f32),
            pltpu.SemaphoreType.DMA,
            pltpu.SemaphoreType.DMA((2,)),
            pltpu.SemaphoreType.DMA((20,)),
            pltpu.SemaphoreType.DMA((20,)),
            pltpu.SemaphoreType.DMA((nz,)),
            pltpu.SemaphoreType.DMA((nz,)),
        ],
        compiler_params=pltpu.CompilerParams(
            collective_id=0, has_side_effects=True, vmem_limit_bytes=40 * 1024 * 1024),
    )(*(pltpu.with_memory_space_constraint(x, pltpu.HBM) for x in (field, transfer, light_angles)))


def solution(mesh):
    sizes = tuple(mesh.shape[name] for name in ("gx", "gy", "gz"))
    placed = (P(None, "gz", "gx", "gy"), P(), P())
    return jax.shard_map(
        functools.partial(shards, sizes), mesh=mesh, in_specs=placed,
        out_specs=P(None, ("gx", "gz"), "gy"), check_vma=False
    )
```

```python
import functools
import math

import jax
import jax.numpy as jnp
from jax import lax
from jax.experimental import pallas as pl
from jax.experimental.pallas import tpu as pltpu
from jax.sharding import PartitionSpec as P

MESH = pl.DeviceIdType.MESH
SIGMA_TAPS = 1.2
OPTICAL = 2.0
SHADE_FLOOR = 0.25
EDGE = 8


def filter_taps():
    places = [-3, -2, -1, 0, 1, 2, 3]
    bell = [math.exp(-place * place / (2.0 * SIGMA_TAPS * SIGMA_TAPS)) for place in places]
    bell_total = sum(bell)
    slope_total = sum((place * place * weight for place, weight in zip(places, bell)))
    smooth_taps = [weight / bell_total for weight in bell]
    slope_taps = [place * weight / slope_total for place, weight in zip(places, bell)]
    return (smooth_taps, slope_taps)


def smooth_of(at):
    taps, _ = filter_taps()
    total = taps[3] * at(0)
    for o in (1, 2, 3):
        total = total + taps[3 + o] * (at(o) + at(-o))
    return total


def slope_of(at):
    _, taps = filter_taps()
    total = taps[4] * (at(1) - at(-1))
    for o in (2, 3):
        total = total + taps[3 + o] * (at(o) - at(-o))
    return total


def both_of(at):
    smooth, slope = filter_taps()
    plain, steep = smooth[3] * at(0), None
    for o in (1, 2, 3):
        after, before = at(o), at(-o)
        plain = plain + smooth[3 + o] * (after + before)
        term = slope[3 + o] * (after - before)
        steep = term if steep is None else steep + term
    return plain, steep


def kernel(sizes, depth_step, field, transfer_in, angles_in, out, transfer, angles, box, own_strips, rim_strips, got_own, got_rim, joined,
           rows_done, flat_done, table, light, inner, stage, slabs,
           local_sem, small_sem, send_sem, recv_sem, slab_send, slab_recv):
    nx, ny, nz = sizes
    _, depth, rows, lanes = field.shape
    total = rows + 2 * EDGE
    ix, iy, iz = (lax.axis_index(name) for name in ("gx", "gy", "gz"))
    spots = (("gx", ix, nx), ("gy", iy, ny), ("gz", iz, nz))

    def has(way):
        need = None
        for (_, place, count), step in zip(spots, way):
            if step:
                here = place > 0 if step < 0 else place < count - 1
                need = here if need is None else jnp.logical_and(need, here)
        return need

    def target(way):
        return {name: place + step for (name, place, _), step in zip(spots, way) if step}

    def lies(axis, step):
        return tuple(step if k == axis else 0 for k in range(3))

    flat_ways = [(dx, dy, 0) for dx in (-1, 0, 1) for dy in (-1, 0, 1) if dx or dy]
    sides = (-1, 1)

    barrier = pltpu.get_barrier_semaphore()
    for way in flat_ways:
        @pl.when(has(way))
        def _():
            pl.semaphore_signal(barrier, inc=1, device_id=target(way), device_id_type=MESH)
    for j in range(1, nz):
        pl.semaphore_signal(barrier, inc=1, device_id={"gz": lax.rem(iz + j, nz)}, device_id_type=MESH)

    own = pltpu.make_async_copy(
        field, box.at[:, pl.ds(3, depth), pl.ds(EDGE, rows), :], local_sem)
    own.start()
    small = (pltpu.make_async_copy(transfer_in, transfer, small_sem.at[0]),
             pltpu.make_async_copy(angles_in, angles, small_sem.at[1]))
    for each in small:
        each.start()

    for step in sides:
        edge = 0 if step < 0 else EDGE + rows
        @pl.when(jnp.logical_not(has(lies(0, step))))
        def _():
            box[:, :, edge:edge + EDGE, :] = jnp.zeros((2, depth + 6, EDGE, lanes), jnp.float32)
            got_own[:, :, edge:edge + EDGE, :] = jnp.zeros((2, 2, EDGE, lanes), jnp.float32)
        first = 0 if step < 0 else depth + 3
        @pl.when(jnp.logical_not(has(lies(2, step))))
        def _():
            flat_done[:, first:first + 3] = jnp.zeros((4, 3, rows, lanes), jnp.float32)
        side = 0 if step < 0 else 1
        @pl.when(jnp.logical_not(has(lies(1, step))))
        def _():
            got_own[side] = jnp.zeros((2, total, lanes), jnp.float32)

    links = {}

    def link(name, way, src, dst, need=None):
        links[name, way] = (len(links), src, dst, need)

    def wanted(name, way):
        need, more = has(way), links[name, way][3]
        return need if more is None else jnp.logical_and(need, more)

    def copy(name, way):
        slot, src, dst, _ = links[name, way]
        return pltpu.make_async_remote_copy(
            src_ref=src, dst_ref=dst, send_sem=send_sem.at[slot], recv_sem=recv_sem.at[slot],
            device_id=target(way), device_id_type=MESH)

    def begin(name, way):
        @pl.when(wanted(name, way))
        def _():
            copy(name, way).start()

    def sent(name, way):
        @pl.when(wanted(name, way))
        def _():
            copy(name, way).wait_send()

    def got(name, way):
        back = tuple(-step for step in way)
        need, more = has(way), links[name, back][3]
        @pl.when(need if more is None else jnp.logical_and(need, more))
        def _():
            copy(name, back).wait_recv()

    every = pl.ds(3, depth)
    middle = pl.ds(EDGE, rows)

    def rows_from(dx):
        return middle if dx == 0 else pl.ds(EDGE if dx < 0 else rows, EDGE)

    def rows_to(dx):
        return middle if dx == 0 else pl.ds(EDGE + rows if dx < 0 else 0, EDGE)

    for way in flat_ways:
        if way[1]:
            side = 0 if way[1] > 0 else 1
            link("strips", way, own_strips.at[:, rows_from(way[0]), :], got_own.at[side, :, rows_to(way[0]), :])
    for step in sides:
        row = 0 if step < 0 else rows - EDGE
        link("rows", lies(0, step), field.at[:, :, pl.ds(row, EDGE), :], box.at[:, every, rows_to(step), :])
        plane = 0 if step < 0 else depth - 3
        to = depth + 3 if step < 0 else 0
        link("planes", lies(2, step), field.at[:, pl.ds(plane, 3)], box.at[:, pl.ds(to, 3), middle, :])
        for name, at, side in (("low", 0, -1), ("high", EDGE + rows, 1)):
            link(name, lies(2, step), box.at[:, pl.ds(3 + plane, 3), pl.ds(at, EDGE), :],
                 box.at[:, pl.ds(to, 3), pl.ds(at, EDGE), :], has(lies(0, side)))
        link("rims", lies(2, step), rim_strips.at[0 if step < 0 else 1], got_rim.at[0 if step > 0 else 1])

    count = nz - 1
    for way in flat_ways:
        count = count + has(way).astype(jnp.int32)

    lane = lax.broadcasted_iota(jnp.int32, (total, lanes), 1)

    def in_group(lane, group):
        return jnp.bitwise_and(lane + (3 + lanes) - 8 * group, lanes - 1) < 6

    pl.semaphore_wait(barrier, count)
    for step in sides:
        begin("planes", lies(2, step))
    for step in sides:
        begin("rows", lies(0, step))
    own.wait()
    group_count = 4 if depth % 4 == 0 else 1

    def pack(i, kept):
        for p in range(group_count):
            z = i * group_count + p
            mask = in_group(lane[:rows], z)
            kept = tuple(
                jnp.where(mask, pltpu.roll(box[v, 3 + z, EDGE:EDGE + rows, :], 8 * z, 1), kept[v])
                for v in range(2))
        return kept

    empty = jnp.zeros((rows, lanes), jnp.float32)
    packed = lax.fori_loop(0, depth // group_count, pack, (empty, empty))
    for v in range(2):
        own_strips[v, EDGE:EDGE + rows, :] = packed[v]

    strip_ways = [way for way in flat_ways if way[1]]
    for way in strip_ways:
        begin("strips", way)

    for each in small:
        each.wait()
    azimuth = jnp.full(light.shape[1:], angles[0], jnp.float32)
    polar = jnp.full(light.shape[1:], angles[1], jnp.float32)
    light[0] = jnp.cos(azimuth) * jnp.sin(polar)
    light[1] = jnp.sin(azimuth) * jnp.sin(polar)
    light[2] = jnp.cos(polar)
    for c in range(4):
        line = jnp.broadcast_to(transfer[c:c + 1, :], table.shape[1:])
        table[2 * c] = line
        table[2 * c + 1] = pltpu.roll(line, lanes - 1, 1) - line

    def merged(left, right):
        here = jnp.bitwise_and(lax.broadcasted_iota(jnp.int32, left.shape, 1), 7)
        return jnp.where(here >= 4, left, right)

    def along_y(v, plane, at, count, group, strips):
        here = lane[:count]
        block = box[v, plane, at:at + count, :]
        halo = pltpu.roll(strips, lanes - 8 * group, 1)

        def place(o):
            if o == 0:
                return block
            if o > 0:
                return pltpu.roll(jnp.where(here < o, halo, block), lanes - o, 1)
            return pltpu.roll(jnp.where(here >= lanes + o, halo, block), -o, 1)

        return both_of(place) if v == 0 else (smooth_of(place),)

    def own_y(blocks, planes):
        def turn(i, carry):
            done = []
            for p in range(planes):
                z = i * planes + p
                for at, count in blocks:
                    found = []
                    for v in range(2):
                        found += along_y(v, z + 3, at, count, z, joined[v, at:at + count, :])
                    done.append((z + 3, at, count, found))
            for plane, at, count, found in done:
                for k in range(3):
                    rows_done[k, plane, at:at + count, :] = found[k]
            return carry
        lax.fori_loop(0, depth // planes, turn, 0)

    def along_x(plane):
        width = 32 if rows % 32 == 0 else EDGE
        for at in range(0, rows, width):
            def reader(k):
                return lambda o: rows_done[k, plane, EDGE + at + o:EDGE + at + o + width, :]
            plain, steep = both_of(reader(0))
            crossed, other = smooth_of(reader(1)), smooth_of(reader(2))
            for k, found in enumerate((plain, steep, crossed, other)):
                flat_done[k, plane, at:at + width, :] = found

    def own_x(z, carry):
        along_x(z + 3)
        return carry

    for step, name in ((-1, "low"), (1, "high")):
        got("rows", lies(0, step))
        for side in sides:
            begin(name, lies(2, side))
    for way in strip_ways:
        got("strips", way)
    for v in range(2):
        joined[v] = merged(got_own[0, v], got_own[1, v])
    for step in sides:
        plane = 0 if step < 0 else depth - 3
        second = jnp.logical_and(lane >= 40, lane < 104)
        rim_strips[0 if step < 0 else 1] = jnp.where(
            second, pltpu.roll(joined[1], (8 * (8 - plane)) % lanes, 1),
            pltpu.roll(joined[0], (8 * (lanes // 8 - plane)) % lanes, 1))
        begin("rims", lies(2, step))
    own_y([(at, 40) for at in range(0, total, 40)], 1)
    lax.fori_loop(0, depth, own_x, 0)

    rims = {-1: ((0, 0), (1, 1), (2, 2)), 1: tuple((h, depth + 3 + h) for h in range(3))}

    def sample(z, at, chunk):
        def reader(k):
            return lambda o: flat_done[k, z + 3 + o, pl.ds(at, chunk), :]
        value, grad_z = both_of(reader(0))
        grad_x = smooth_of(reader(1))
        grad_y = smooth_of(reader(2))
        mixture = smooth_of(reader(3))
        position = 0.5 * (lanes - 1) + (0.5 * (lanes - 1)) * jnp.tanh(0.5 * value)
        index = jnp.minimum(position.astype(jnp.int32), lanes - 2)
        share = position - index.astype(jnp.float32)

        def look(c):
            low = jnp.take_along_axis(table[2 * c, :chunk], index, axis=1, mode="promise_in_bounds")
            rise = jnp.take_along_axis(table[2 * c + 1, :chunk], index, axis=1, mode="promise_in_bounds")
            return low + share * rise

        facing = grad_x * light[0, :chunk] + grad_y * light[1, :chunk] + grad_z * light[2, :chunk]
        square = grad_x * grad_x + grad_y * grad_y + grad_z * grad_z + SHADE_FLOOR
        shade = 0.25 + 0.75 * (facing * facing / square)
        alpha = 1.0 - jnp.exp((-0.5 * OPTICAL * depth_step) * look(3) * (1.0 + jnp.tanh(0.5 * mixture)))
        lit = alpha * shade
        return (lit * look(0), lit * look(1), lit * look(2), alpha)

    def over(front, back):
        left = 1.0 - front[3]
        return tuple(f + left * b for f, b in zip(front, back))

    def nothing(chunk):
        return tuple(jnp.zeros((chunk, lanes), jnp.float32) for _ in range(4))

    wide = light.shape[1]

    height = rows // nz
    inner_rows = min(height, wide)

    def inner_slab(slab):
        def inner_chunk(c, carry):
            at = pl.multiple_of(slab * height + c * inner_rows, inner_rows)

            def turn(i, acc):
                z = 3 + 2 * i
                pair = [sample(z + p, at, inner_rows) for p in range(2)]
                return over(acc, over(*pair))

            result = lax.fori_loop(0, (depth - 6) // 2, turn, nothing(inner_rows))
            for k in range(4):
                inner[k, pl.ds(at, inner_rows), :] = result[k]
            return carry

        lax.fori_loop(0, height // inner_rows, inner_chunk, 0)

    for j in range(1, nz + 1):
        inner_slab(lax.rem(iz + j, nz))

    for step in sides:
        for name in ("planes", "low", "high", "rims"):
            got(name, lies(2, step))

    for step in sides:
        @pl.when(has(lies(2, step)))
        def _():
            for h, plane in rims[step]:
                for at in range(0, total, 40):
                    found = []
                    for v in range(2):
                        found += along_y(v, plane, at, 40, 8 * v + h, got_rim[0 if step < 0 else 1, at:at + 40, :])
                    for k in range(3):
                        rows_done[k, plane, at:at + 40, :] = found[k]
            for h, plane in rims[step]:
                along_x(plane)

    def slab_copy(j):
        return pltpu.make_async_remote_copy(
            src_ref=stage.at[j - 1], dst_ref=slabs.at[iz], send_sem=slab_send.at[j - 1],
            recv_sem=slab_recv.at[iz], device_id={"gz": lax.rem(iz + j, nz)}, device_id_type=MESH)

    for j in range(1, nz + 1):
        slab = lax.rem(iz + j, nz)

        at = pl.multiple_of(slab * height, height)
        acc = sample(0, at, height)
        for z in (1, 2):
            acc = over(acc, sample(z, at, height))
        acc = over(acc, tuple(inner[k, pl.ds(at, height), :] for k in range(4)))
        for z in range(depth - 3, depth):
            acc = over(acc, sample(z, at, height))
        for k in range(4):
            if j < nz:
                stage[j - 1, k] = acc[k]
            else:
                slabs[iz, k] = acc[k]
        if j < nz:
            slab_copy(j).start()

    for j in range(1, nz):
        source = lax.rem(iz + j, nz)
        pltpu.make_async_remote_copy(
            src_ref=stage.at[j - 1], dst_ref=slabs.at[source], send_sem=slab_send.at[j - 1],
            recv_sem=slab_recv.at[source], device_id={"gz": source}, device_id_type=MESH).wait_recv()

    image = tuple(slabs[0, k] for k in range(4))
    for k in range(1, nz):
        image = over(image, tuple(slabs[k, c] for c in range(4)))
    for c in range(4):
        out[c] = image[c]

    for name, way in links:
        sent(name, way)
    for j in range(1, nz):
        slab_copy(j).wait_send()


def shards(sizes, field, transfer, light_angles):
    nx, ny, nz = sizes
    _, depth, rows, lanes = field.shape
    total = rows + 2 * EDGE
    height = rows // nz
    chunk = 32
    full = depth + 6
    f32 = jnp.float32
    return pl.pallas_call(
        functools.partial(kernel, sizes, 1.0 / (depth * nz)),
        out_shape=jax.ShapeDtypeStruct((4, height, lanes), f32),
        in_specs=[
            pl.BlockSpec(memory_space=pltpu.HBM),
            pl.BlockSpec(memory_space=pltpu.HBM),
            pl.BlockSpec(memory_space=pltpu.HBM),
        ],
        out_specs=pl.BlockSpec(memory_space=pltpu.VMEM),
        scratch_shapes=[
            pltpu.VMEM((4, lanes), f32),
            pltpu.SMEM((2,), f32),
            pltpu.VMEM((2, full, total, lanes), f32),
            pltpu.VMEM((2, total, lanes), f32),
            pltpu.VMEM((2, total, lanes), f32),
            pltpu.VMEM((2, 2, total, lanes), f32),
            pltpu.VMEM((2, total, lanes), f32),
            pltpu.VMEM((2, total, lanes), f32),
            pltpu.VMEM((3, full, total, lanes), f32),
            pltpu.VMEM((4, full, rows, lanes), f32),
            pltpu.VMEM((8, chunk, lanes), f32),
            pltpu.VMEM((3, chunk, lanes), f32),
            pltpu.VMEM((4, rows, lanes), f32),
            pltpu.VMEM((nz - 1, 4, height, lanes), f32),
            pltpu.VMEM((nz, 4, height, lanes), f32),
            pltpu.SemaphoreType.DMA,
            pltpu.SemaphoreType.DMA((2,)),
            pltpu.SemaphoreType.DMA((20,)),
            pltpu.SemaphoreType.DMA((20,)),
            pltpu.SemaphoreType.DMA((nz,)),
            pltpu.SemaphoreType.DMA((nz,)),
        ],
        compiler_params=pltpu.CompilerParams(
            collective_id=0, has_side_effects=True, vmem_limit_bytes=40 * 1024 * 1024),
    )(*(pltpu.with_memory_space_constraint(x, pltpu.HBM) for x in (field, transfer, light_angles)))


def solution(mesh):
    sizes = tuple(mesh.shape[name] for name in ("gx", "gy", "gz"))
    placed = (P(None, "gz", "gx", "gy"), P(), P())
    return jax.shard_map(
        functools.partial(shards, sizes), mesh=mesh, in_specs=placed,
        out_specs=P(None, ("gx", "gz"), "gy"), check_vma=False
    )
```
